256 devices in a mesh: wide: 64 (over y, x, z_hi, core), narrow: 4 (over z_lo).
Axes of the slice: x: 4, y: 4, z: 8 (z_hi: 2, z_lo: 4; z = z_hi * 4 + z_lo), core: 2. Of those that a mesh axis runs over, the one named last changes fastest.
Arguments:
- field: bfloat16 [64, 4, 1024, 1024], P('narrow', None, 'wide'), may hold values from -6 to 6
- spectral_weight: bfloat16 [64, 64, 64, 128], P('narrow', None, 'wide'), may hold values from -0.5 to 0.5
- cotangent: bfloat16 [64, 4, 1024, 1024], P('narrow', None, 'wide'), may hold values from -1.5 to 1.5
Outputs:
- output: bfloat16 [64, 4, 1024, 1024], P('narrow', None, 'wide')
- weight_grad: float32 [64, 64, 64, 128], P('narrow', None, 'wide')
- field_grad: bfloat16 [64, 4, 1024, 1024], P('narrow', None, 'wide')
The draws below stay inside these ranges and needn't reach their ends.
All inputs are finite; a program needn't handle non-finite values.
Results may differ from the reference program's by a relative error of at most 0.012.
Values may be sent and summed in bfloat16 or wider, within the bound.
A program may use at most 64 MiB of HBM per device.

```python
import math
import jax
import jax.numpy as jnp
from jax import lax

C = 64
X = 1024
Y = 1024
MX = 64
MY = 64
ZS = 4


def steps_of(stream_key, shape, shards, low, top_value):
    def one(position, shards_of):
        steps = jax.random.uniform(jax.random.fold_in(jax.random.fold_in(stream_key, 6), position), (shards_of,), jnp.float32, low / len(shards), top_value / len(shards))
        return jnp.repeat(jnp.exp(steps), shape[position] // shards_of).reshape((-1,) + (1,) * (len(shape) - position - 1))

    loudness = one(*shards[0])
    for cut in shards[1:]:
        loudness = loudness * one(*cut)
    return loudness


def normal_values(stream_key, dims, width, most, pieces=(), held_as=jnp.bfloat16):
    array = width * jax.random.normal(stream_key, dims, jnp.float32)
    if pieces:
        array = array * steps_of(stream_key, dims, pieces, -0.22, 0.18)
    return jnp.clip(array, -most, most).astype(held_as)


def setup_inputs(seed: int = 0) -> dict:
    streams_of = jax.random.split(jax.random.key(seed), 4)
    field = normal_values(streams_of[0], (C, ZS, Y, X), 1.0, 6.0, ((0, 4), (2, 64)))
    spectral_weight = normal_values(streams_of[1], (C, C, MX, 2 * MY), (2 * C) ** -0.5, 0.5, ((0, 4), (2, 64)))
    cotangent = normal_values(streams_of[2], (C, ZS, Y, X), 0.25, 1.5, ((0, 4), (2, 64)))
    return dict(field=field, spectral_weight=spectral_weight, cotangent=cotangent)


def angle_table(freqs, length):
    places = jnp.arange(length, dtype=jnp.int32)
    phase = (places[:, None] * freqs[None, :]) % length
    return phase.astype(jnp.float32) * (2.0 * math.pi / length)


def fourier_tables():
    kx_freqs = jnp.arange(MX, dtype=jnp.int32)
    ky_index = jnp.arange(MY, dtype=jnp.int32)
    ky_freqs = jnp.where(ky_index < MY // 2, ky_index, ky_index - MY + Y).astype(jnp.int32)
    angle_x = angle_table(kx_freqs, X)
    cos_x, sin_x = jnp.cos(angle_x), jnp.sin(angle_x)
    forward_x = (jnp.stack([cos_x, -sin_x], axis=-1).reshape(X, 2 * MX) / 32.0).astype(jnp.bfloat16)
    inverse_x = (jnp.transpose(jnp.stack([cos_x, -sin_x], axis=-1), (1, 2, 0)).reshape(2 * MX, X) / 4.0).astype(jnp.bfloat16)
    angle_y = angle_table(ky_freqs, Y)
    cos_y, sin_y = jnp.cos(angle_y), jnp.sin(angle_y)
    upper = jnp.concatenate([cos_y, -sin_y], axis=1)
    lower = jnp.concatenate([sin_y, cos_y], axis=1)
    forward_y = (jnp.concatenate([upper, lower], axis=0) / 32.0).astype(jnp.bfloat16)
    first = jnp.concatenate([cos_y.T, sin_y.T], axis=1)
    second = jnp.concatenate([-sin_y.T, cos_y.T], axis=1)
    inverse_y = (jnp.concatenate([first, second], axis=0) / 32.0).astype(jnp.bfloat16)
    return forward_x, inverse_x, forward_y, inverse_y


def contract(form, left, right):
    return jnp.einsum(form, left.astype(jnp.float32), right.astype(jnp.float32))


def reference(field, spectral_weight, cotangent):
    forward_x, inverse_x, forward_y, inverse_y = fourier_tables()
    x_modes = lax.map(lambda plane: contract('zyx,xf->zfy', plane, forward_x).astype(jnp.bfloat16), field)
    spectra = contract('czkp,pm->czkm', x_modes.reshape(C, ZS, MX, 2 * Y), forward_y).astype(jnp.bfloat16)
    real_spec, imag_spec = spectra[..., :MY], spectra[..., MY:]
    real_weight, imag_weight = spectral_weight[..., :MY], spectral_weight[..., MY:]
    mix_form = 'izkm,iokm->ozkm'
    real_out = contract(mix_form, real_spec, real_weight) - contract(mix_form, imag_spec, imag_weight)
    imag_out = contract(mix_form, imag_spec, real_weight) + contract(mix_form, real_spec, imag_weight)
    mixed = jnp.concatenate([real_out, imag_out], axis=-1).astype(jnp.bfloat16)
    y_back = contract('czkm,mp->czkp', mixed, inverse_y).astype(jnp.bfloat16).reshape(C, ZS, 2 * MX, Y)
    output = lax.map(lambda plane: contract('zfy,fx->zyx', plane, inverse_x).astype(jnp.bfloat16), y_back)
    cot_x = lax.map(lambda plane: contract('zyx,fx->zfy', plane, inverse_x).astype(jnp.bfloat16), cotangent)
    cot_modes = contract('czkp,mp->czkm', cot_x.reshape(C, ZS, MX, 2 * Y), inverse_y).astype(jnp.bfloat16)
    real_cot, imag_cot = cot_modes[..., :MY], cot_modes[..., MY:]
    grad_form = 'izkm,ozkm->iokm'
    grad_real = contract(grad_form, real_spec, real_cot) + contract(grad_form, imag_spec, imag_cot)
    grad_imag = contract(grad_form, real_spec, imag_cot) - contract(grad_form, imag_spec, real_cot)
    weight_grad = jnp.concatenate([grad_real, grad_imag], axis=-1)
    back_form = 'iokm,ozkm->izkm'
    spec_real = contract(back_form, real_weight, real_cot) + contract(back_form, imag_weight, imag_cot)
    spec_imag = contract(back_form, real_weight, imag_cot) - contract(back_form, imag_weight, real_cot)
    spec_grad = jnp.concatenate([spec_real, spec_imag], axis=-1).astype(jnp.bfloat16)
    grad_modes = contract('czkm,pm->czkp', spec_grad, forward_y).astype(jnp.bfloat16).reshape(C, ZS, 2 * MX, Y)
    field_grad = lax.map(lambda plane: contract('zfy,xf->zyx', plane, forward_x).astype(jnp.bfloat16), grad_modes)
    return output, weight_grad, field_grad
```

```python
import math

import jax
import jax.numpy as jnp
import ml_dtypes
import numpy as np
from jax import lax
from jax.experimental import pallas as pl
from jax.experimental.pallas import tpu as pltpu
from jax.sharding import PartitionSpec as P

X = 1024
Y = 1024
MX = 64
MY = 64
GROUP = 32
ROWS = 1024
MESH = pl.DeviceIdType.MESH
F32 = jnp.float32
BF16 = jnp.bfloat16


def mode_of(group, half):
    return (group // 2) * 4 + half * 2 + group % 2


def tables():
    step = np.float32(2.0 * math.pi / X)
    group = np.arange(GROUP)
    k = np.stack([mode_of(group, h) for h in range(2)], axis=1)
    ax = ((np.arange(X)[:, None, None] * k[None]) % X).astype(np.float32) * step
    fx = np.stack([np.cos(ax), -np.sin(ax)], axis=-1).reshape(X, 2 * MX)
    forward_x = (fx / np.float32(32)).astype(ml_dtypes.bfloat16)
    inverse_x = np.ascontiguousarray((fx / np.float32(4)).astype(ml_dtypes.bfloat16).T)
    m = np.arange(MY)
    q = np.where(m < MY // 2, m, m - MY + Y)
    ay = ((np.arange(Y)[:, None] * q[None]) % Y).astype(np.float32) * step
    cos, sin = np.cos(ay), np.sin(ay)
    fy = np.stack([np.concatenate([cos, -sin], 1), np.concatenate([sin, cos], 1)], 0)
    fy = (fy / np.float32(32)).astype(ml_dtypes.bfloat16)
    halves = []
    for h in range(2):
        y = 16 * mode_of(group, h)[:, None] + np.arange(16)[None]
        part = fy[:, y, :].reshape(2, GROUP, 2, 8, 2 * MY)
        halves.append(part.transpose(1, 0, 3, 2, 4).reshape(GROUP * 16, 4 * MY))
    return forward_x, inverse_x, np.stack(halves)


def halves_swapped(a):
    return pltpu.roll(a, MY, a.ndim - 1)


def low_lanes(shape):
    return lax.broadcasted_iota(jnp.int32, shape, len(shape) - 1) < MY


def exchange_kernel(
    field, cot, weight, fx_hbm, fy_hbm,
    back_out, grad_out, wg_out,
    rows_in, fx, fy, wt, w1, w2, xm, t32, send1, recv1, part, part_in, s_rows, a1, a2,
    mixpart, mix_in, cots, d1, d2, sg, modes, send2, recv2, wg,
    in_sem, s1_send, s1_recv, px_send, px_recv, rs_send, rs_recv, ag_send, ag_recv,
    mx_send, mx_recv, s2_send, s2_recv, wg_sem,
):
    w = lax.axis_index("wide")
    n = lax.axis_index("narrow")
    half = lax.rem(lax.div(w, 2), 2)
    g = lax.div(w, 4) * 2 + lax.rem(w, 2)
    partner = {"wide": w + 2 - 4 * half, "narrow": n}

    def member(i):
        other = lax.rem(g + i, GROUP)
        wide = lax.div(other, 2) * 4 + half * 2 + lax.rem(other, 2)
        return other, {"wide": wide, "narrow": n}

    def aside(i):
        other = lax.rem(n + i, 4)
        return other, {"wide": w, "narrow": other}

    chunk = ROWS // 4
    copies = []
    copies.append(pltpu.make_async_copy(fx_hbm, fx, in_sem.at[8]))
    for a, src in enumerate((field, cot)):
        for c in range(4):
            rows = pl.ds(c * chunk, chunk)
            copies.append(
                pltpu.make_async_copy(src.at[rows], rows_in.at[a, rows], in_sem.at[a * 4 + c])
            )
    fy_copy = pltpu.make_async_copy(fy_hbm.at[half], fy, in_sem.at[9])
    wt_copy = pltpu.make_async_copy(weight, wt, in_sem.at[10])
    for copy in copies:
        copy.start()
    fy_copy.start()
    wt_copy.start()

    barrier = pltpu.get_barrier_semaphore()

    def greet(i, _):
        pl.semaphore_signal(barrier, 1, device_id=member(i)[1], device_id_type=MESH)
        return 0

    lax.fori_loop(1, GROUP, greet, 0)
    pl.semaphore_signal(barrier, 1, device_id=partner, device_id_type=MESH)
    for i in range(1, 4):
        pl.semaphore_signal(barrier, 1, device_id=aside(i)[1], device_id_type=MESH)

    copies[0].wait()

    def all_to_all(src, dst, send_sem, recv_sem):
        def one(i, _):
            other, device = member(i)
            pltpu.make_async_remote_copy(
                src.at[other], dst.at[g], send_sem, recv_sem, device_id=device, device_id_type=MESH
            ).start()
            return 0

        lax.fori_loop(1, GROUP, one, 0)
        dst[g] = src[g]

    def wait_blocks(ref, count, sem):
        block = ref.at[pl.ds(0, count)]
        pltpu.make_async_copy(block, block, sem).wait()

    for a in range(2):
        for c in range(4):
            copies[1 + a * 4 + c].wait()
            rows = pl.ds(c * chunk, chunk)
            xm[rows, :] = jnp.dot(rows_in[a, rows, :], fx[...], preferred_element_type=F32)

        def turn(y8, _):
            pieces = [
                xm[pl.ds(z * 16 + y2 * 8 + y8, 16, stride=64), :]
                for y2 in range(2)
                for z in range(4)
            ]
            t32[pl.ds(y8, 128, stride=8), :] = jnp.concatenate(pieces, axis=0).T
            return 0

        lax.fori_loop(0, 8, turn, 0)
        send1[a] = t32[...].astype(BF16).reshape(GROUP, 32, 128)
        if a == 0:
            pl.semaphore_wait(barrier, GROUP - 1 + 1 + 3)
        all_to_all(send1.at[a], recv1.at[a], s1_send.at[a], s1_recv.at[a])

    wt_copy.wait()

    def spread(i, _):
        both = wt[i].astype(F32)
        turned = halves_swapped(both)
        low = low_lanes(both.shape)
        w1[i] = jnp.where(low, both, turned)
        w2[i] = jnp.where(low, turned, both)
        return 0

    lax.fori_loop(0, 16, spread, 0)
    fy_copy.wait()

    to_partner = []
    for a in range(2):
        wait_blocks(recv1.at[a], GROUP - 1, s1_recv.at[a])
        for h in range(2):
            block = recv1[a, :, h * 16 : (h + 1) * 16, :].reshape(GROUP * 16, 128)
            both = lax.dot_general(
                block, fy[...], (((0,), (0,)), ((), ())), preferred_element_type=F32
            )
            part[a, h] = both[:64, :128] + both[64:, 128:]
        copy = pltpu.make_async_remote_copy(
            part.at[a, 1 - half], part_in.at[a], px_send.at[a], px_recv.at[a],
            device_id=partner, device_id_type=MESH,
        )
        copy.start()
        to_partner.append(copy)

    low = low_lanes((64, 128))

    to_partner[0].wait_recv()
    spectra = (part[0, half] + part_in[0]).astype(BF16).astype(F32)
    turned = halves_swapped(spectra)
    s_rows[0] = spectra
    s_rows[1] = jnp.where(low, -turned, turned)
    a1[...] = jnp.where(low, spectra, turned)
    a2[...] = jnp.where(low, turned, spectra)
    for z in range(4):

        def mix(i, total):
            return (
                total
                + w1[i] * s_rows[0, pl.ds(z * 16 + i, 1), :]
                + w2[i] * s_rows[1, pl.ds(z * 16 + i, 1), :]
            )

        total = lax.fori_loop(0, 16, mix, jnp.zeros((64, 128), F32))
        mixpart[:, z] = total.reshape(4, 16, 128)
    for i in range(1, 4):
        other, device = aside(i)
        pltpu.make_async_remote_copy(
            mixpart.at[other], mix_in.at[i - 1], rs_send, rs_recv, device_id=device, device_id_type=MESH
        ).start()

    to_partner[1].wait_recv()
    cots[n] = ((part[1, half] + part_in[1]) * 8.0).astype(BF16).reshape(4, 16, 128)
    for i in range(1, 4):
        other, device = aside(i)
        pltpu.make_async_remote_copy(
            cots.at[n], cots.at[n], ag_send, ag_recv, device_id=device, device_id_type=MESH
        ).start()

    back = []

    def to_half(a):
        copy = pltpu.make_async_remote_copy(
            modes.at[a, half], modes.at[a, half], mx_send.at[a], mx_recv.at[a],
            device_id=partner, device_id_type=MESH,
        )
        copy.start()
        back.append(copy)

    wait_blocks(mix_in, 3, rs_recv)
    mixed = mixpart[n] + mix_in[0] + mix_in[1] + mix_in[2]
    modes[0, half] = mixed.astype(BF16).reshape(64, 128)
    to_half(0)

    wait_blocks(cots, 3, ag_recv)
    for o in range(4):
        for z in range(4):
            d = cots[o, z].astype(F32)
            turned = halves_swapped(d)
            d1[z, o * 16 : (o + 1) * 16, :] = d
            d2[z, o * 16 : (o + 1) * 16, :] = jnp.where(low_lanes((16, 128)), turned, -turned)

    def gradient(i, _):
        for z in range(4):
            sums = jnp.sum(w1[i] * d1[z] + w2[i] * d2[z], axis=0, keepdims=True)
            sg[pl.ds(z * 16 + i, 1), :] = sums
        return 0

    lax.fori_loop(0, 16, gradient, 0)
    modes[1, half] = (sg[...] * 0.125).astype(BF16)
    to_half(1)

    for a in range(2):
        back[a].wait_recv()
        for h in range(2):
            m = modes[a, h]
            zero = jnp.zeros_like(m)
            wide = jnp.concatenate(
                [jnp.concatenate([m, zero], axis=1), jnp.concatenate([zero, m], axis=1)], axis=0
            )
            rows = lax.dot_general(
                fy[...], wide, (((1,), (1,)), ((), ())), preferred_element_type=F32
            )
            send2[a, :, h * 16 : (h + 1) * 16, :] = rows.astype(BF16).reshape(GROUP, 16, 128)
        all_to_all(send2.at[a], recv2.at[a], s2_send.at[a], s2_recv.at[a])

    def weight_gradient(i, _):
        total = jnp.zeros((64, 128), F32)
        for z in range(4):
            row = pl.ds(z * 16 + i, 1)
            total += a1[row, :] * d1[z] + a2[row, :] * d2[z]
        wg[i] = total
        return 0

    lax.fori_loop(0, 16, weight_gradient, 0)
    wg_copy = pltpu.make_async_copy(wg, wg_out, wg_sem)
    wg_copy.start()

    for a, out in enumerate((back_out, grad_out)):
        wait_blocks(recv2.at[a], GROUP - 1, s2_recv.at[a])
        t32[...] = recv2[a].reshape(ROWS, 128).astype(F32)

        def turn_back(y8, _):
            block = t32[pl.ds(y8, 128, stride=8), :].T
            for y2 in range(2):
                for z in range(4):
                    at = (y2 * 4 + z) * 16
                    xm[pl.ds(z * 16 + y2 * 8 + y8, 16, stride=64), :] = block[at : at + 16]
            return 0

        lax.fori_loop(0, 8, turn_back, 0)
        out[...] = xm[...].astype(BF16)

    wg_copy.wait()
    for a in range(2):
        wait_blocks(send1.at[a], GROUP - 1, s1_send.at[a])
        wait_blocks(send2.at[a], GROUP - 1, s2_send.at[a])
        to_partner[a].wait_send()
        back[a].wait_send()
    wait_blocks(mix_in, 3, rs_send)
    wait_blocks(cots, 3, ag_send)


def exchange(field, cot, weight, fx, fy):
    any_spec = pl.BlockSpec(memory_space=pl.ANY)
    vmem = pl.BlockSpec(memory_space=pltpu.VMEM)
    dma = pltpu.SemaphoreType.DMA
    return pl.pallas_call(
        exchange_kernel,
        out_shape=(
            jax.ShapeDtypeStruct((ROWS, 128), BF16),
            jax.ShapeDtypeStruct((ROWS, 128), BF16),
            jax.ShapeDtypeStruct((16, 64, 128), F32),
        ),
        in_specs=[any_spec] * 5,
        out_specs=(vmem, vmem, any_spec),
        scratch_shapes=[
            pltpu.VMEM((2, ROWS, X), BF16),
            pltpu.VMEM((X, 128), BF16),
            pltpu.VMEM((GROUP * 16, 256), BF16),
            pltpu.VMEM((16, 64, 128), BF16),
            pltpu.VMEM((16, 64, 128), F32),
            pltpu.VMEM((16, 64, 128), F32),
            pltpu.VMEM((ROWS, 128), F32),
            pltpu.VMEM((ROWS, 128), F32),
            pltpu.VMEM((2, GROUP, 32, 128), BF16),
            pltpu.VMEM((2, GROUP, 32, 128), BF16),
            pltpu.VMEM((2, 2, 64, 128), F32),
            pltpu.VMEM((2, 64, 128), F32),
            pltpu.VMEM((2, 64, 128), F32),
            pltpu.VMEM((64, 128), F32),
            pltpu.VMEM((64, 128), F32),
            pltpu.VMEM((4, 4, 16, 128), F32),
            pltpu.VMEM((3, 4, 16, 128), F32),
            pltpu.VMEM((4, 4, 16, 128), BF16),
            pltpu.VMEM((4, 64, 128), F32),
            pltpu.VMEM((4, 64, 128), F32),
            pltpu.VMEM((64, 128), F32),
            pltpu.VMEM((2, 2, 64, 128), BF16),
            pltpu.VMEM((2, GROUP, 32, 128), BF16),
            pltpu.VMEM((2, GROUP, 32, 128), BF16),
            pltpu.VMEM((16, 64, 128), F32),
            dma((11,)),
            dma((2,)),
            dma((2,)),
            dma((2,)),
            dma((2,)),
            dma,
            dma,
            dma,
            dma,
            dma((2,)),
            dma((2,)),
            dma((2,)),
            dma((2,)),
            dma,
        ],
        compiler_params=pltpu.CompilerParams(
            collective_id=0, has_side_effects=True, vmem_limit_bytes=40 << 20
        ),
    )(field, cot, weight, fx, fy)


def rows_kernel(back, grad, ix, out, fgrad, buf, sem):
    chunk = ROWS // 4
    copies = []
    for a, (src, dst) in enumerate(((back, out), (grad, fgrad))):
        for c in range(4):
            rows = pl.ds(c * chunk, chunk)
            buf[a, rows, :] = jnp.dot(
                src[rows, :], ix[...], preferred_element_type=F32
            ).astype(BF16)
            copy = pltpu.make_async_copy(buf.at[a, rows], dst.at[rows], sem.at[a * 4 + c])
            copy.start()
            copies.append(copy)
    for copy in copies:
        copy.wait()


def rows_back(back, grad, ix):
    any_spec = pl.BlockSpec(memory_space=pl.ANY)
    vmem = pl.BlockSpec(memory_space=pltpu.VMEM)
    return pl.pallas_call(
        rows_kernel,
        out_shape=(jax.ShapeDtypeStruct((ROWS, X), BF16),) * 2,
        in_specs=[vmem] * 3,
        out_specs=(any_spec, any_spec),
        scratch_shapes=[pltpu.VMEM((2, ROWS, X), BF16), pltpu.SemaphoreType.DMA((8,))],
        compiler_params=pltpu.CompilerParams(vmem_limit_bytes=24 << 20),
    )(back, grad, ix)


def solution(mesh):
    forward_x, inverse_x, forward_y = tables()

    def body(field, spectral_weight, cotangent):
        shape = field.shape
        back, grad, weight_grad = exchange(
            field.reshape(ROWS, X),
            cotangent.reshape(ROWS, X),
            spectral_weight.reshape(16, 64, 128),
            jnp.asarray(forward_x),
            jnp.asarray(forward_y),
        )
        output, field_grad = rows_back(back, grad, jnp.asarray(inverse_x))
        return (
            output.reshape(shape),
            weight_grad.reshape(16, 64, 1, 128),
            field_grad.reshape(shape),
        )

    spec = P("narrow", None, "wide", None)
    return jax.shard_map(
        body, mesh=mesh, in_specs=(spec,) * 3, out_specs=(spec,) * 3, check_vma=False
    )
```

```python
import math

import jax
import jax.numpy as jnp
import ml_dtypes
import numpy as np
from jax import lax
from jax.experimental import pallas as pl
from jax.experimental.pallas import tpu as pltpu
from jax.sharding import PartitionSpec as P

X = 1024
Y = 1024
MX = 64
MY = 64
GROUP = 32
ROWS = 1024
MESH = pl.DeviceIdType.MESH
F32 = jnp.float32
BF16 = jnp.bfloat16


def mode_of(group, half):
    return (group // 2) * 4 + half * 2 + group % 2


def tables():
    step = np.float32(2.0 * math.pi / X)
    group = np.arange(GROUP)
    k = np.stack([mode_of(group, h) for h in range(2)], axis=1)
    ax = ((np.arange(X)[:, None, None] * k[None]) % X).astype(np.float32) * step
    fx = np.stack([np.cos(ax), -np.sin(ax)], axis=-1).reshape(X, 2 * MX)
    forward_x = (fx / np.float32(32)).astype(ml_dtypes.bfloat16)
    inverse_x = np.ascontiguousarray((fx / np.float32(4)).astype(ml_dtypes.bfloat16).T)
    m = np.arange(MY)
    q = np.where(m < MY // 2, m, m - MY + Y)
    ay = ((np.arange(Y)[:, None] * q[None]) % Y).astype(np.float32) * step
    cos, sin = np.cos(ay), np.sin(ay)
    fy = np.stack([np.concatenate([cos, -sin], 1), np.concatenate([sin, cos], 1)], 0)
    fy = (fy / np.float32(32)).astype(ml_dtypes.bfloat16)
    halves = []
    for h in range(2):
        y = 16 * mode_of(group, h)[:, None] + np.arange(16)[None]
        part = fy[:, y, :].reshape(2, GROUP, 2, 8, 2 * MY)
        halves.append(part.transpose(1, 0, 3, 2, 4).reshape(GROUP * 16, 4 * MY))
    return forward_x, inverse_x, np.stack(halves)


def halves_swapped(a):
    return pltpu.roll(a, MY, a.ndim - 1)


def low_lanes(shape):
    return lax.broadcasted_iota(jnp.int32, shape, len(shape) - 1) < MY


def exchange_kernel(
    field, cot, weight, fx_hbm, fy_hbm,
    back_out, grad_out, wg_out,
    rows_in, fx, fy, wt, w1, w2, xm, t32, send1, recv1, part, part_in, s_rows, a1, a2,
    mixpart, mix_in, cots, d1, d2, sg, modes, send2, recv2, wg,
    in_sem, s1_send, s1_recv, px_send, px_recv, rs_send, rs_recv, ag_send, ag_recv,
    mx_send, mx_recv, s2_send, s2_recv, wg_sem,
):
    w = lax.axis_index("wide")
    n = lax.axis_index("narrow")
    half = lax.rem(lax.div(w, 2), 2)
    g = lax.div(w, 4) * 2 + lax.rem(w, 2)
    partner = {"wide": w + 2 - 4 * half, "narrow": n}

    def member(i):
        other = lax.rem(g + i, GROUP)
        wide = lax.div(other, 2) * 4 + half * 2 + lax.rem(other, 2)
        return other, {"wide": wide, "narrow": n}

    def aside(i):
        other = lax.rem(n + i, 4)
        return other, {"wide": w, "narrow": other}

    chunk = ROWS // 4
    copies = []
    copies.append(pltpu.make_async_copy(fx_hbm, fx, in_sem.at[8]))
    for a, src in enumerate((field, cot)):
        for c in range(4):
            rows = pl.ds(c * chunk, chunk)
            copies.append(
                pltpu.make_async_copy(src.at[rows], rows_in.at[a, rows], in_sem.at[a * 4 + c])
            )
    fy_copy = pltpu.make_async_copy(fy_hbm.at[half], fy, in_sem.at[9])
    wt_copy = pltpu.make_async_copy(weight, wt, in_sem.at[10])
    for copy in copies:
        copy.start()
    fy_copy.start()
    wt_copy.start()

    barrier = pltpu.get_barrier_semaphore()

    def greet(i, _):
        pl.semaphore_signal(barrier, 1, device_id=member(i)[1], device_id_type=MESH)
        return 0

    lax.fori_loop(1, GROUP, greet, 0)
    pl.semaphore_signal(barrier, 1, device_id=partner, device_id_type=MESH)
    for i in range(1, 4):
        pl.semaphore_signal(barrier, 1, device_id=aside(i)[1], device_id_type=MESH)

    copies[0].wait()

    def all_to_all(src, dst, send_sem, recv_sem):
        def one(i, _):
            other, device = member(i)
            pltpu.make_async_remote_copy(
                src.at[other], dst.at[g], send_sem, recv_sem, device_id=device, device_id_type=MESH
            ).start()
            return 0

        lax.fori_loop(1, GROUP, one, 0)
        dst[g] = src[g]

    def wait_blocks(ref, count, sem):
        block = ref.at[pl.ds(0, count)]
        pltpu.make_async_copy(block, block, sem).wait()

    for a in range(2):
        for c in range(4):
            copies[1 + a * 4 + c].wait()
            rows = pl.ds(c * chunk, chunk)
            xm[rows, :] = jnp.dot(rows_in[a, rows, :], fx[...], preferred_element_type=F32)

        def turn(y8, _):
            pieces = [
                xm[pl.ds(z * 16 + y2 * 8 + y8, 16, stride=64), :]
                for y2 in range(2)
                for z in range(4)
            ]
            t32[pl.ds(y8, 128, stride=8), :] = jnp.concatenate(pieces, axis=0).T
            return 0

        lax.fori_loop(0, 8, turn, 0, unroll=True)
        send1[a] = t32[...].astype(BF16).reshape(GROUP, 32, 128)
        if a == 0:
            pl.semaphore_wait(barrier, GROUP - 1 + 1 + 3)
        all_to_all(send1.at[a], recv1.at[a], s1_send.at[a], s1_recv.at[a])

    wt_copy.wait()

    def spread(i, _):
        both = wt[i].astype(F32)
        turned = halves_swapped(both)
        low = low_lanes(both.shape)
        w1[i] = jnp.where(low, both, turned)
        w2[i] = jnp.where(low, turned, both)
        return 0

    lax.fori_loop(0, 16, spread, 0, unroll=2)
    fy_copy.wait()

    low = low_lanes((64, 128))

    def sums_over_y(a):
        wait_blocks(recv1.at[a], GROUP - 1, s1_recv.at[a])
        for h in range(2):
            block = recv1[a, :, h * 16 : (h + 1) * 16, :].reshape(GROUP * 16, 128)
            both = lax.dot_general(
                block, fy[...], (((0,), (0,)), ((), ())), preferred_element_type=F32
            )
            part[a, h] = both[:64, :128] + both[64:, 128:]
        copy = pltpu.make_async_remote_copy(
            part.at[a, 1 - half], part_in.at[a], px_send.at[a], px_recv.at[a],
            device_id=partner, device_id_type=MESH,
        )
        copy.start()
        return copy

    def to_half(a):
        copy = pltpu.make_async_remote_copy(
            modes.at[a, half], modes.at[a, half], mx_send.at[a], mx_recv.at[a],
            device_id=partner, device_id_type=MESH,
        )
        copy.start()
        return copy

    field_part = sums_over_y(0)
    field_part.wait_recv()
    spectra = (part[0, half] + part_in[0]).astype(BF16).astype(F32)
    turned = halves_swapped(spectra)
    s_rows[0] = spectra
    s_rows[1] = jnp.where(low, -turned, turned)
    a1[...] = jnp.where(low, spectra, turned)
    a2[...] = jnp.where(low, turned, spectra)
    for o in range(2):

        def mix(i, totals):
            x1, x2 = w1[i, o * 32 : (o + 1) * 32, :], w2[i, o * 32 : (o + 1) * 32, :]
            return tuple(
                total
                + x1 * s_rows[0, pl.ds(z * 16 + i, 1), :]
                + x2 * s_rows[1, pl.ds(z * 16 + i, 1), :]
                for z, total in enumerate(totals)
            )

        totals = lax.fori_loop(0, 16, mix, (jnp.zeros((32, 128), F32),) * 4, unroll=4)
        for z, total in enumerate(totals):
            mixpart[o * 2 : (o + 1) * 2, z] = total.reshape(2, 16, 128)
    for i in range(1, 4):
        other, device = aside(i)
        pltpu.make_async_remote_copy(
            mixpart.at[other], mix_in.at[i - 1], rs_send, rs_recv, device_id=device, device_id_type=MESH
        ).start()

    cot_part = sums_over_y(1)

    wait_blocks(mix_in, 3, rs_recv)
    mixed = mixpart[n] + mix_in[0] + mix_in[1] + mix_in[2]
    modes[0, half] = mixed.astype(BF16).reshape(64, 128)
    field_back = to_half(0)

    cot_part.wait_recv()
    cots[n] = ((part[1, half] + part_in[1]) * 8.0).astype(BF16).reshape(4, 16, 128)
    for i in range(1, 4):
        other, device = aside(i)
        pltpu.make_async_remote_copy(
            cots.at[n], cots.at[n], ag_send, ag_recv, device_id=device, device_id_type=MESH
        ).start()

    def rows_of_y(a, copy):
        copy.wait_recv()
        for h in range(2):
            m = modes[a, h]
            zero = jnp.zeros_like(m)
            wide = jnp.concatenate(
                [jnp.concatenate([m, zero], axis=1), jnp.concatenate([zero, m], axis=1)], axis=0
            )
            rows = lax.dot_general(
                fy[...], wide, (((1,), (1,)), ((), ())), preferred_element_type=F32
            )
            send2[a, :, h * 16 : (h + 1) * 16, :] = rows.astype(BF16).reshape(GROUP, 16, 128)
        all_to_all(send2.at[a], recv2.at[a], s2_send.at[a], s2_recv.at[a])

    rows_of_y(0, field_back)

    wait_blocks(cots, 3, ag_recv)
    for o in range(4):
        for z in range(4):
            d = cots[o, z].astype(F32)
            turned = halves_swapped(d)
            d1[z, o * 16 : (o + 1) * 16, :] = d
            d2[z, o * 16 : (o + 1) * 16, :] = jnp.where(low_lanes((16, 128)), turned, -turned)

    def gradient(i, _):
        x1, x2 = w1[i], w2[i]
        for z in range(4):
            sg[pl.ds(z * 16 + i, 1), :] = jnp.sum(x1 * d1[z] + x2 * d2[z], axis=0, keepdims=True)
        return 0

    lax.fori_loop(0, 16, gradient, 0, unroll=2)
    modes[1, half] = (sg[...] * 0.125).astype(BF16)
    cot_back = to_half(1)
    rows_of_y(1, cot_back)

    def weight_gradient(i, _):
        for o in range(2):
            total = jnp.zeros((32, 128), F32)
            for z in range(4):
                row = pl.ds(z * 16 + i, 1)
                outs = slice(o * 32, (o + 1) * 32)
                total += a1[row, :] * d1[z, outs, :] + a2[row, :] * d2[z, outs, :]
            wg[i, o * 32 : (o + 1) * 32, :] = total
        return 0

    lax.fori_loop(0, 16, weight_gradient, 0, unroll=2)
    wg_copy = pltpu.make_async_copy(wg, wg_out, wg_sem)
    wg_copy.start()

    for a, out in enumerate((back_out, grad_out)):
        wait_blocks(recv2.at[a], GROUP - 1, s2_recv.at[a])
        t32[...] = recv2[a].reshape(ROWS, 128).astype(F32)

        def turn_back(y8, _):
            block = t32[pl.ds(y8, 128, stride=8), :].T
            for y2 in range(2):
                for z in range(4):
                    at = (y2 * 4 + z) * 16
                    xm[pl.ds(z * 16 + y2 * 8 + y8, 16, stride=64), :] = block[at : at + 16]
            return 0

        lax.fori_loop(0, 8, turn_back, 0, unroll=True)
        out[...] = xm[...].astype(BF16)

    for a, (first, second) in enumerate(((field_part, field_back), (cot_part, cot_back))):
        wait_blocks(send1.at[a], GROUP - 1, s1_send.at[a])
        wait_blocks(send2.at[a], GROUP - 1, s2_send.at[a])
        first.wait_send()
        second.wait_send()
    wg_copy.wait()
    wait_blocks(mix_in, 3, rs_send)
    wait_blocks(cots, 3, ag_send)


def exchange(field, cot, weight, fx, fy):
    hbm = pl.BlockSpec(memory_space=pltpu.HBM)
    vmem = pl.BlockSpec(memory_space=pltpu.VMEM)
    dma = pltpu.SemaphoreType.DMA
    return pl.pallas_call(
        exchange_kernel,
        out_shape=(
            jax.ShapeDtypeStruct((ROWS, 128), BF16),
            jax.ShapeDtypeStruct((ROWS, 128), BF16),
            jax.ShapeDtypeStruct((16, 64, 128), F32),
        ),
        in_specs=[hbm] * 5,
        out_specs=(vmem, vmem, hbm),
        scratch_shapes=[
            pltpu.VMEM((2, ROWS, X), BF16),
            pltpu.VMEM((X, 128), BF16),
            pltpu.VMEM((GROUP * 16, 256), BF16),
            pltpu.VMEM((16, 64, 128), BF16),
            pltpu.VMEM((16, 64, 128), F32),
            pltpu.VMEM((16, 64, 128), F32),
            pltpu.VMEM((ROWS, 128), F32),
            pltpu.VMEM((ROWS, 128), F32),
            pltpu.VMEM((2, GROUP, 32, 128), BF16),
            pltpu.VMEM((2, GROUP, 32, 128), BF16),
            pltpu.VMEM((2, 2, 64, 128), F32),
            pltpu.VMEM((2, 64, 128), F32),
            pltpu.VMEM((2, 64, 128), F32),
            pltpu.VMEM((64, 128), F32),
            pltpu.VMEM((64, 128), F32),
            pltpu.VMEM((4, 4, 16, 128), F32),
            pltpu.VMEM((3, 4, 16, 128), F32),
            pltpu.VMEM((4, 4, 16, 128), BF16),
            pltpu.VMEM((4, 64, 128), F32),
            pltpu.VMEM((4, 64, 128), F32),
            pltpu.VMEM((64, 128), F32),
            pltpu.VMEM((2, 2, 64, 128), BF16),
            pltpu.VMEM((2, GROUP, 32, 128), BF16),
            pltpu.VMEM((2, GROUP, 32, 128), BF16),
            pltpu.VMEM((16, 64, 128), F32),
            dma((11,)),
            dma((2,)),
            dma((2,)),
            dma((2,)),
            dma((2,)),
            dma,
            dma,
            dma,
            dma,
            dma((2,)),
            dma((2,)),
            dma((2,)),
            dma((2,)),
            dma,
            ],
        compiler_params=pltpu.CompilerParams(
            collective_id=0, has_side_effects=True, vmem_limit_bytes=55836672
        ),
    )(field, cot, weight, fx, fy)


def rows_kernel(back, grad, wg, ix, out, wg_out, fgrad, buf, sem):
    chunk = ROWS // 4
    copies = [pltpu.make_async_copy(wg, wg_out, sem.at[8])]
    copies[0].start()
    for a, (src, dst) in enumerate(((back, out), (grad, fgrad))):
        for c in range(4):
            rows = pl.ds(c * chunk, chunk)
            buf[a, rows, :] = jnp.dot(
                src[rows, :], ix[...], preferred_element_type=F32
            ).astype(BF16)
            copy = pltpu.make_async_copy(buf.at[a, rows], dst.at[rows], sem.at[a * 4 + c])
            copy.start()
            copies.append(copy)
    for copy in copies:
        copy.wait()


def rows_back(back, grad, wg, ix):
    hbm = pl.BlockSpec(memory_space=pltpu.HBM)
    vmem = pl.BlockSpec(memory_space=pltpu.VMEM)
    rows = jax.ShapeDtypeStruct((ROWS, X), BF16)
    return pl.pallas_call(
        rows_kernel,
        out_shape=(rows, jax.ShapeDtypeStruct((ROWS, 128), F32), rows),
        in_specs=[vmem, vmem, hbm, vmem],
        out_specs=(hbm,) * 3,
        scratch_shapes=[pltpu.VMEM((2, ROWS, X), BF16), pltpu.SemaphoreType.DMA((9,))],
        compiler_params=pltpu.CompilerParams(vmem_limit_bytes=55574528),
    )(back, grad, wg, ix)


def solution(mesh):
    forward_x, inverse_x, forward_y = tables()

    def body(field, spectral_weight, cotangent):
        shape = field.shape
        back, grad, weight_grad = exchange(
            field.reshape(ROWS, X),
            cotangent.reshape(ROWS, X),
            spectral_weight.reshape(16, 64, 128),
            jnp.asarray(forward_x),
            jnp.asarray(forward_y),
        )
        output, weight_grad, field_grad = rows_back(
            back, grad, weight_grad.reshape(ROWS, 128), jnp.asarray(inverse_x)
        )
        return (
            output.reshape(shape),
            weight_grad.reshape(16, 64, 1, 128),
            field_grad.reshape(shape),
        )

    spec = P("narrow", None, "wide", None)
    return jax.shard_map(
        body, mesh=mesh, in_specs=(spec,) * 3, out_specs=(spec,) * 3, check_vma=False
    )
```

```python
import math

import jax
import jax.numpy as jnp
import ml_dtypes
import numpy as np
from jax import lax
from jax.experimental import pallas as pl
from jax.experimental.pallas import tpu as pltpu
from jax.sharding import PartitionSpec as P

X = 1024
Y = 1024
MX = 64
MY = 64
GROUP = 32
ROWS = 1024
MESH = pl.DeviceIdType.MESH
F32 = jnp.float32
BF16 = jnp.bfloat16


def mode_of(group, half):
    return (group // 2) * 4 + half * 2 + group % 2


def tables():
    step = np.float32(2.0 * math.pi / X)
    group = np.arange(GROUP)
    k = np.stack([mode_of(group, h) for h in range(2)], axis=1)
    ax = ((np.arange(X)[:, None, None] * k[None]) % X).astype(np.float32) * step
    fx = np.stack([np.cos(ax), -np.sin(ax)], axis=-1).reshape(X, 2 * MX)
    forward_x = (fx / np.float32(32)).astype(ml_dtypes.bfloat16)
    inverse_x = np.ascontiguousarray((fx / np.float32(4)).astype(ml_dtypes.bfloat16).T)
    m = np.arange(MY)
    q = np.where(m < MY // 2, m, m - MY + Y)
    ay = ((np.arange(Y)[:, None] * q[None]) % Y).astype(np.float32) * step
    cos, sin = np.cos(ay), np.sin(ay)
    fy = np.stack([np.concatenate([cos, -sin], 1), np.concatenate([sin, cos], 1)], 0)
    fy = (fy / np.float32(32)).astype(ml_dtypes.bfloat16)
    halves = []
    for h in range(2):
        y = 16 * mode_of(group, h)[:, None] + np.arange(16)[None]
        part = fy[:, y, :].reshape(2, GROUP, 2, 8, 2 * MY)
        halves.append(part.transpose(1, 0, 3, 2, 4).reshape(GROUP * 16, 4 * MY))
    return forward_x, inverse_x, np.stack(halves)


def halves_swapped(a):
    return pltpu.roll(a, MY, a.ndim - 1)


def low_lanes(shape):
    return lax.broadcasted_iota(jnp.int32, shape, len(shape) - 1) < MY


def spread_cots(cots, d1, d2):
    for o in range(4):
        for z in range(4):
            d = cots[o, z].astype(F32)
            turned = halves_swapped(d)
            d1[z, o * 16 : (o + 1) * 16, :] = d
            d2[z, o * 16 : (o + 1) * 16, :] = jnp.where(low_lanes((16, 128)), turned, -turned)


def far_first():
    offsets = [(dy, dx, dc) for dy in range(4) for dx in range(4) for dc in range(2)]
    return sorted(offsets[1:], key=lambda o: -(min(o[0], 4 - o[0]) + min(o[1], 4 - o[1])))


RING = (4, 3, 5, 2, 6, 1, 7)
COT, FIELD = 0, 1


def exchange_kernel(
    cot, field, weight, fx_hbm, fy_hbm,
    grad_out, back_out, spectra_out, cots,
    rows_in, fx, fy, wt, w1, w2, xm, t32, send1, recv1, part, part_f32, part_in, s_rows,
    mixpart, mix_in, cots_in, d1, d2, sg, modes, send2, recv2,
    in_sem, s1_send, s1_recv, px_send, px_recv, mix_send, mix_recv, cots_send, cots_recv,
    mx_send, mx_recv, s2_send, s2_recv,
):
    w = lax.axis_index("wide")
    n = lax.axis_index("narrow")
    at_y, at_x, half, core = lax.div(w, 16), lax.rem(lax.div(w, 4), 4), lax.rem(lax.div(w, 2), 2), lax.rem(w, 2)
    g = lax.div(w, 4) * 2 + core
    at_z = half * 4 + n
    partner = {"wide": w + 2 - 4 * half, "narrow": n}

    def member(offset):
        dy, dx, dc = offset
        chip = lax.rem(at_y + dy, 4) * 4 + lax.rem(at_x + dx, 4)
        to_core = lax.rem(core + dc, 2)
        return chip * 2 + to_core, {"wide": chip * 4 + half * 2 + to_core, "narrow": n}

    def along_z(offset):
        z = lax.rem(at_z + offset, 8)
        to_half, to_n = lax.div(z, 4), lax.rem(z, 4)
        return to_half, to_n, {"wide": w + 2 * (to_half - half), "narrow": to_n}

    chunk = ROWS // 4
    copies = []
    copies.append(pltpu.make_async_copy(fx_hbm, fx, in_sem.at[8]))
    for a, src in enumerate((cot, field)):
        for c in range(4):
            rows = pl.ds(c * chunk, chunk)
            copies.append(
                pltpu.make_async_copy(src.at[rows], rows_in.at[a, rows], in_sem.at[a * 4 + c])
            )
    fy_copy = pltpu.make_async_copy(fy_hbm.at[half], fy, in_sem.at[9])
    wt_copy = pltpu.make_async_copy(weight, wt, in_sem.at[10])
    for copy in copies:
        copy.start()
    fy_copy.start()
    wt_copy.start()

    barrier = pltpu.get_barrier_semaphore()
    for offset in far_first():
        pl.semaphore_signal(barrier, 1, device_id=member(offset)[1], device_id_type=MESH)
    for offset in RING:
        pl.semaphore_signal(barrier, 1, device_id=along_z(offset)[2], device_id_type=MESH)

    copies[0].wait()

    def all_to_all(src, dst, send_sem, recv_sem):
        for offset in far_first():
            other, device = member(offset)
            pltpu.make_async_remote_copy(
                src.at[other], dst.at[g], send_sem, recv_sem, device_id=device, device_id_type=MESH
            ).start()
        dst[g] = src[g]

    def wait_blocks(ref, count, sem):
        block = ref.at[pl.ds(0, count)]
        pltpu.make_async_copy(block, block, sem).wait()

    def x_transform(a):
        for c in range(4):
            copies[1 + a * 4 + c].wait()
            rows = pl.ds(c * chunk, chunk)
            xm[a, rows, :] = jnp.dot(rows_in[a, rows, :], fx[...], preferred_element_type=F32)

    def blocks_for_modes(a):
        def turn(y8, _):
            pieces = [
                xm[a, pl.ds(z * 16 + y2 * 8 + y8, 16, stride=64), :]
                for y2 in range(2)
                for z in range(4)
            ]
            t32[pl.ds(y8, 128, stride=8), :] = jnp.concatenate(pieces, axis=0).T
            return 0

        lax.fori_loop(0, 8, turn, 0, unroll=True)
        send1[a] = t32[...].astype(BF16).reshape(GROUP, 32, 128)

    x_transform(COT)
    blocks_for_modes(COT)
    x_transform(FIELD)
    pl.semaphore_wait(barrier, GROUP - 1 + 7)
    all_to_all(send1.at[COT], recv1.at[COT], s1_send.at[COT], s1_recv.at[COT])
    blocks_for_modes(FIELD)
    all_to_all(send1.at[FIELD], recv1.at[FIELD], s1_send.at[FIELD], s1_recv.at[FIELD])

    wt_copy.wait()

    def spread(i, _):
        both = wt[i].astype(F32)
        turned = halves_swapped(both)
        low = low_lanes(both.shape)
        w1[i] = jnp.where(low, both, turned)
        w2[i] = jnp.where(low, turned, both)
        return 0

    lax.fori_loop(0, 16, spread, 0, unroll=2)
    fy_copy.wait()

    def sums_over_y(a):
        wait_blocks(recv1.at[a], GROUP - 1, s1_recv.at[a])
        for h in range(2):
            block = recv1[a, :, h * 16 : (h + 1) * 16, :].reshape(GROUP * 16, 128)
            both = lax.dot_general(
                block, fy[...], (((0,), (0,)), ((), ())), preferred_element_type=F32
            )
            sums = both[:64, :128] + both[64:, 128:]
            if a == FIELD:
                part_f32[h] = sums
            part[a, h] = sums.astype(BF16)

    sums_over_y(COT)
    for offset in RING:
        to_half, _, device = along_z(offset)
        pltpu.make_async_remote_copy(
            part.at[COT, to_half], cots_in.at[at_z], cots_send, cots_recv, device_id=device, device_id_type=MESH
        ).start()
    cots_in[at_z] = part[COT, half]

    sums_over_y(FIELD)
    field_part = pltpu.make_async_remote_copy(
        part.at[FIELD, 1 - half], part_in, px_send, px_recv, device_id=partner, device_id_type=MESH
    )
    field_part.start()

    wait_blocks(cots_in, 7, cots_recv)
    for o in range(4):
        both = cots_in[o].astype(F32) + cots_in[4 + o].astype(F32)
        cots[o] = (both * 8.0).astype(BF16).reshape(4, 16, 128)
    spread_cots(cots, d1, d2)

    def gradient(i, _):
        x1, x2 = w1[i], w2[i]
        for z in range(4):
            sg[pl.ds(z * 16 + i, 1), :] = jnp.sum(x1 * d1[z] + x2 * d2[z], axis=0, keepdims=True)
        return 0

    lax.fori_loop(0, 16, gradient, 0, unroll=2)
    modes[COT, half] = (sg[...] * 0.125).astype(BF16)
    cot_back = pltpu.make_async_remote_copy(
        modes.at[COT, half], modes.at[COT, half], mx_send, mx_recv, device_id=partner, device_id_type=MESH
    )
    cot_back.start()

    field_part.wait_recv()
    low = low_lanes((64, 128))
    spectra = (part_f32[half] + part_in[...].astype(F32)).astype(BF16).astype(F32)
    turned = halves_swapped(spectra)
    s_rows[0] = spectra
    s_rows[1] = jnp.where(low, -turned, turned)
    spectra_out[...] = spectra
    for o in range(2):

        def mix(i, totals):
            x1, x2 = w1[i, o * 32 : (o + 1) * 32, :], w2[i, o * 32 : (o + 1) * 32, :]
            return tuple(
                total
                + x1 * s_rows[0, pl.ds(z * 16 + i, 1), :]
                + x2 * s_rows[1, pl.ds(z * 16 + i, 1), :]
                for z, total in enumerate(totals)
            )

        totals = lax.fori_loop(0, 16, mix, (jnp.zeros((32, 128), F32),) * 4, unroll=4)
        for z, total in enumerate(totals):
            for k in range(2):
                mixpart[o * 2 + k, z * 16 : (z + 1) * 16, :] = total[k * 16 : (k + 1) * 16].astype(BF16)
    for offset in RING:
        _, to_n, device = along_z(offset)
        pltpu.make_async_remote_copy(
            mixpart.at[to_n], mix_in.at[at_z], mix_send, mix_recv, device_id=device, device_id_type=MESH
        ).start()
    mix_in[at_z] = mixpart[n]

    def rows_of_y(a):
        for h in range(2):
            m = modes[a, h]
            zero = jnp.zeros_like(m)
            wide = jnp.concatenate(
                [jnp.concatenate([m, zero], axis=1), jnp.concatenate([zero, m], axis=1)], axis=0
            )
            rows = lax.dot_general(
                fy[...], wide, (((1,), (1,)), ((), ())), preferred_element_type=F32
            )
            send2[a, :, h * 16 : (h + 1) * 16, :] = rows.astype(BF16).reshape(GROUP, 16, 128)
        all_to_all(send2.at[a], recv2.at[a], s2_send.at[a], s2_recv.at[a])

    cot_back.wait_recv()
    rows_of_y(COT)

    wait_blocks(mix_in, 7, mix_recv)
    for h in range(2):
        total = mix_in[h * 4].astype(F32)
        for k in range(1, 4):
            total += mix_in[h * 4 + k].astype(F32)
        modes[FIELD, h] = total.astype(BF16)
    rows_of_y(FIELD)

    for a, out in ((COT, grad_out), (FIELD, back_out)):
        wait_blocks(recv2.at[a], GROUP - 1, s2_recv.at[a])
        t32[...] = recv2[a].reshape(ROWS, 128).astype(F32)

        def turn_back(y8, _):
            block = t32[pl.ds(y8, 128, stride=8), :].T
            for y2 in range(2):
                for z in range(4):
                    at = (y2 * 4 + z) * 16
                    xm[a, pl.ds(z * 16 + y2 * 8 + y8, 16, stride=64), :] = block[at : at + 16]
            return 0

        lax.fori_loop(0, 8, turn_back, 0, unroll=True)
        out[...] = xm[a].astype(BF16)

    for a in range(2):
        wait_blocks(send1.at[a], GROUP - 1, s1_send.at[a])
        wait_blocks(send2.at[a], GROUP - 1, s2_send.at[a])
    field_part.wait_send()
    cot_back.wait_send()
    wait_blocks(cots_in, 7, cots_send)
    wait_blocks(mix_in, 7, mix_send)


def exchange(cot, field, weight, fx, fy):
    hbm = pl.BlockSpec(memory_space=pltpu.HBM)
    vmem = pl.BlockSpec(memory_space=pltpu.VMEM)
    dma = pltpu.SemaphoreType.DMA
    return pl.pallas_call(
        exchange_kernel,
        out_shape=(
            jax.ShapeDtypeStruct((ROWS, 128), BF16),
            jax.ShapeDtypeStruct((ROWS, 128), BF16),
            jax.ShapeDtypeStruct((64, 128), F32),
            jax.ShapeDtypeStruct((4, 4, 16, 128), BF16),
        ),
        in_specs=[hbm] * 5,
        out_specs=(vmem,) * 4,
        scratch_shapes=[
            pltpu.VMEM((2, ROWS, X), BF16),
            pltpu.VMEM((X, 128), BF16),
            pltpu.VMEM((GROUP * 16, 256), BF16),
            pltpu.VMEM((16, 64, 128), BF16),
            pltpu.VMEM((16, 64, 128), F32),
            pltpu.VMEM((16, 64, 128), F32),
            pltpu.VMEM((2, ROWS, 128), F32),
            pltpu.VMEM((ROWS, 128), F32),
            pltpu.VMEM((2, GROUP, 32, 128), BF16),
            pltpu.VMEM((2, GROUP, 32, 128), BF16),
            pltpu.VMEM((2, 2, 64, 128), BF16),
            pltpu.VMEM((2, 64, 128), F32),
            pltpu.VMEM((64, 128), BF16),
            pltpu.VMEM((2, 64, 128), F32),
            pltpu.VMEM((4, 64, 128), BF16),
            pltpu.VMEM((8, 64, 128), BF16),
            pltpu.VMEM((8, 64, 128), BF16),
            pltpu.VMEM((4, 64, 128), F32),
            pltpu.VMEM((4, 64, 128), F32),
            pltpu.VMEM((64, 128), F32),
            pltpu.VMEM((2, 2, 64, 128), BF16),
            pltpu.VMEM((2, GROUP, 32, 128), BF16),
            pltpu.VMEM((2, GROUP, 32, 128), BF16),
            dma((11,)),
            dma((2,)),
            dma((2,)),
            dma,
            dma,
            dma,
            dma,
            dma,
            dma,
            dma,
            dma,
            dma((2,)),
            dma((2,)),
        ],
        compiler_params=pltpu.CompilerParams(
            collective_id=0, has_side_effects=True, vmem_limit_bytes=55705600
        ),
    )(cot, field, weight, fx, fy)


def rows_kernel(
    back, grad, spectra, cots, ix, out, wg_out, fgrad, buf, a1, a2, d1, d2, wg, sem
):
    chunk = ROWS // 4
    copies = []

    def rows_out(a, src, dst):
        for c in range(4):
            rows = pl.ds(c * chunk, chunk)
            buf[a, rows, :] = jnp.dot(
                src[rows, :], ix[...], preferred_element_type=F32
            ).astype(BF16)
            copy = pltpu.make_async_copy(buf.at[a, rows], dst.at[rows], sem.at[a * 4 + c])
            copy.start()
            copies.append(copy)

    rows_out(0, back, out)

    s = spectra[...]
    turned = halves_swapped(s)
    low = low_lanes((64, 128))
    a1[...] = jnp.where(low, s, turned)
    a2[...] = jnp.where(low, turned, s)
    spread_cots(cots, d1, d2)

    def weight_gradient(i, _):
        for o in range(2):
            total = jnp.zeros((32, 128), F32)
            for z in range(4):
                row = pl.ds(z * 16 + i, 1)
                outs = slice(o * 32, (o + 1) * 32)
                total += a1[row, :] * d1[z, outs, :] + a2[row, :] * d2[z, outs, :]
            wg[pl.ds(pl.multiple_of(i * 64 + o * 32, 32), 32), :] = total
        return 0

    lax.fori_loop(0, 16, weight_gradient, 0, unroll=2)
    copy = pltpu.make_async_copy(wg, wg_out, sem.at[8])
    copy.start()
    copies.append(copy)

    rows_out(1, grad, fgrad)
    for copy in copies:
        copy.wait()


def rows_back(back, grad, spectra, cots, ix):
    hbm = pl.BlockSpec(memory_space=pltpu.HBM)
    vmem = pl.BlockSpec(memory_space=pltpu.VMEM)
    rows = jax.ShapeDtypeStruct((ROWS, X), BF16)
    return pl.pallas_call(
        rows_kernel,
        out_shape=(rows, jax.ShapeDtypeStruct((ROWS, 128), F32), rows),
        in_specs=[vmem] * 5,
        out_specs=(hbm,) * 3,
        scratch_shapes=[
            pltpu.VMEM((2, ROWS, X), BF16),
            pltpu.VMEM((64, 128), F32),
            pltpu.VMEM((64, 128), F32),
            pltpu.VMEM((4, 64, 128), F32),
            pltpu.VMEM((4, 64, 128), F32),
            pltpu.VMEM((ROWS, 128), F32),
            pltpu.SemaphoreType.DMA((9,)),
        ],
        compiler_params=pltpu.CompilerParams(vmem_limit_bytes=55443456),
    )(back, grad, spectra, cots, ix)


def solution(mesh):
    forward_x, inverse_x, forward_y = tables()

    def body(field, spectral_weight, cotangent):
        shape = field.shape
        grad, back, spectra, cots = exchange(
            cotangent.reshape(ROWS, X),
            field.reshape(ROWS, X),
            spectral_weight.reshape(16, 64, 128),
            jnp.asarray(forward_x),
            jnp.asarray(forward_y),
        )
        output, weight_grad, field_grad = rows_back(
            back, grad, spectra, cots, jnp.asarray(inverse_x)
        )
        return (
            output.reshape(shape),
            weight_grad.reshape(16, 64, 1, 128),
            field_grad.reshape(shape),
        )

    spec = P("narrow", None, "wide", None)
    return jax.shard_map(
        body, mesh=mesh, in_specs=(spec,) * 3, out_specs=(spec,) * 3, check_vma=False
    )
```

```python
import math

import jax
import jax.numpy as jnp
import ml_dtypes
import numpy as np
from jax import lax
from jax.experimental import pallas as pl
from jax.experimental.pallas import tpu as pltpu
from jax.sharding import PartitionSpec as P

X = 1024
Y = 1024
MX = 64
MY = 64
GROUP = 32
ROWS = 1024
MESH = pl.DeviceIdType.MESH
F32 = jnp.float32
BF16 = jnp.bfloat16


def mode_of(group, half):
    return (group // 2) * 4 + half * 2 + group % 2


def tables():
    step = np.float32(2.0 * math.pi / X)
    group = np.arange(GROUP)
    k = np.stack([mode_of(group, h) for h in range(2)], axis=1)
    ax = ((np.arange(X)[:, None, None] * k[None]) % X).astype(np.float32) * step
    fx = np.stack([np.cos(ax), -np.sin(ax)], axis=-1).reshape(X, 2 * MX)
    forward_x = (fx / np.float32(32)).astype(ml_dtypes.bfloat16)
    inverse_x = np.ascontiguousarray((fx / np.float32(4)).astype(ml_dtypes.bfloat16).T)
    m = np.arange(MY)
    q = np.where(m < MY // 2, m, m - MY + Y)
    ay = ((np.arange(Y)[:, None] * q[None]) % Y).astype(np.float32) * step
    cos, sin = np.cos(ay), np.sin(ay)
    fy = np.stack([np.concatenate([cos, -sin], 1), np.concatenate([sin, cos], 1)], 0)
    fy = (fy / np.float32(32)).astype(ml_dtypes.bfloat16)
    halves = []
    for h in range(2):
        y = 16 * mode_of(group, h)[:, None] + np.arange(16)[None]
        part = fy[:, y, :].reshape(2, GROUP, 2, 8, 2 * MY)
        halves.append(part.transpose(1, 0, 3, 2, 4).reshape(GROUP * 16, 4 * MY))
    return forward_x, inverse_x, np.stack(halves)


def halves_swapped(a):
    return pltpu.roll(a, MY, a.ndim - 1)


def low_lanes(shape):
    return lax.broadcasted_iota(jnp.int32, shape, len(shape) - 1) < MY


def far_first():
    offsets = [(dy, dx, dc) for dy in range(4) for dx in range(4) for dc in range(2)]
    return sorted(offsets[1:], key=lambda o: -(min(o[0], 4 - o[0]) + min(o[1], 4 - o[1])))


COT, FIELD = 0, 1
FAR, OWN = 0, 1


def exchange_kernel(
    cot, field, weight, fx_hbm, fy_hbm,
    grad_out, back_out, wg,
    rows_in, fx, fy, wt, w1, w2, xm, t32, send1, recv1, part, part_own, part_in, s_rows,
    a1, a2, mixpart, mix_in, cots_in, d1, d2, sg, modes, send2, recv2,
    in_sem, s1_send, s1_recv, px_send, px_recv, mix_send, mix_recv, cots_send, cots_recv,
    mx_send, mx_recv, s2_send, s2_recv,
):
    w = lax.axis_index("wide")
    n = lax.axis_index("narrow")
    at_y, at_x, half, core = lax.div(w, 16), lax.rem(lax.div(w, 4), 4), lax.rem(lax.div(w, 2), 2), lax.rem(w, 2)
    g = lax.div(w, 4) * 2 + core
    at_z = half * 4 + n
    partner = {"wide": w + 2 - 4 * half, "narrow": n}

    def member(offset):
        dy, dx, dc = offset
        chip = lax.rem(at_y + dy, 4) * 4 + lax.rem(at_x + dx, 4)
        to_core = lax.rem(core + dc, 2)
        return chip * 2 + to_core, {"wide": chip * 4 + half * 2 + to_core, "narrow": n}

    modes_of = (1 - half, half)

    def along_z(r):
        wide = w + 2 * (modes_of[r] - half)
        for i in (0, 1, 3, 2) if r == FAR else (2, 1, 3):
            to_n = lax.rem(n + i, 4)
            yield to_n, {"wide": wide, "narrow": to_n}

    chunk = ROWS // 4
    copies = []
    copies.append(pltpu.make_async_copy(fx_hbm, fx, in_sem.at[8]))
    for a, src in enumerate((cot, field)):
        for c in range(4):
            rows = pl.ds(c * chunk, chunk)
            copies.append(
                pltpu.make_async_copy(src.at[rows], rows_in.at[a, rows], in_sem.at[a * 4 + c])
            )
    fy_copy = pltpu.make_async_copy(fy_hbm.at[half], fy, in_sem.at[9])
    wt_copy = pltpu.make_async_copy(weight, wt, in_sem.at[10])
    for copy in copies:
        copy.start()
    fy_copy.start()
    wt_copy.start()

    barrier = pltpu.get_barrier_semaphore()
    for offset in far_first():
        pl.semaphore_signal(barrier, 1, device_id=member(offset)[1], device_id_type=MESH)
    for r in (FAR, OWN):
        for _, device in along_z(r):
            pl.semaphore_signal(barrier, 1, device_id=device, device_id_type=MESH)

    copies[0].wait()

    def all_to_all(a, r, sent, received, send_sem, recv_sem):
        src, dst = sent.at[a, modes_of[r]], received.at[a, modes_of[r]]
        for offset in far_first():
            other, device = member(offset)
            pltpu.make_async_remote_copy(
                src.at[other], dst.at[g], send_sem.at[a, r], recv_sem.at[a, r],
                device_id=device, device_id_type=MESH,
            ).start()
        dst[g] = src[g]

    def wait_blocks(ref, count, sem):
        block = ref.at[pl.ds(0, count)]
        pltpu.make_async_copy(block, block, sem).wait()

    def x_transform(a):
        for c in range(4):
            copies[1 + a * 4 + c].wait()
            rows = pl.ds(c * chunk, chunk)
            xm[a, rows, :] = jnp.dot(rows_in[a, rows, :], fx[...], preferred_element_type=F32)

    def blocks_for_modes(a):
        def turn(y8, _):
            pieces = [
                xm[a, pl.ds(z * 16 + y2 * 8 + y8, 16, stride=64), :]
                for y2 in range(2)
                for z in range(4)
            ]
            t32[pl.ds(y8, 128, stride=8), :] = jnp.concatenate(pieces, axis=0).T
            return 0

        lax.fori_loop(0, 8, turn, 0, unroll=True)
        blocks = t32[...].astype(BF16).reshape(GROUP, 2, 16, 128)
        for h in range(2):
            send1[a, h] = blocks[:, h]

    x_transform(COT)
    blocks_for_modes(COT)
    x_transform(FIELD)
    pl.semaphore_wait(barrier, GROUP - 1 + 7)
    all_to_all(COT, FAR, send1, recv1, s1_send, s1_recv)
    blocks_for_modes(FIELD)
    all_to_all(FIELD, FAR, send1, recv1, s1_send, s1_recv)
    all_to_all(COT, OWN, send1, recv1, s1_send, s1_recv)
    all_to_all(FIELD, OWN, send1, recv1, s1_send, s1_recv)

    wt_copy.wait()

    def spread(i, _):
        both = wt[i].astype(F32)
        turned = halves_swapped(both)
        low = low_lanes(both.shape)
        w1[i] = jnp.where(low, both, turned)
        w2[i] = jnp.where(low, turned, both)
        return 0

    lax.fori_loop(0, 16, spread, 0, unroll=2)
    fy_copy.wait()

    def sums_over_y(a, r):
        wait_blocks(recv1.at[a, 0], GROUP - 1, s1_recv.at[a, r])
        block = recv1[a, modes_of[r]].reshape(GROUP * 16, 128)
        both = lax.dot_general(
            block, fy[...], (((0,), (0,)), ((), ())), preferred_element_type=F32
        )
        return both[:64, :128] + both[64:, 128:]

    def cots_along_z(r):
        part[COT, r] = sums_over_y(COT, r).astype(BF16)
        for _, device in along_z(r):
            pltpu.make_async_remote_copy(
                part.at[COT, r], cots_in.at[at_z], cots_send.at[r], cots_recv.at[r],
                device_id=device, device_id_type=MESH,
            ).start()

    cots_along_z(FAR)

    part[FIELD, FAR] = sums_over_y(FIELD, FAR).astype(BF16)
    field_part = pltpu.make_async_remote_copy(
        part.at[FIELD, FAR], part_in, px_send, px_recv, device_id=partner, device_id_type=MESH
    )
    field_part.start()

    cots_along_z(OWN)
    cots_in[at_z] = part[COT, OWN]
    part_own[...] = sums_over_y(FIELD, OWN)

    field_part.wait_recv()
    low = low_lanes((64, 128))
    spectra = (part_own[...] + part_in[...].astype(F32)).astype(BF16).astype(F32)
    turned = halves_swapped(spectra)
    s_rows[0] = spectra
    s_rows[1] = jnp.where(low, -turned, turned)
    a1[...] = jnp.where(low, spectra, turned)
    a2[...] = jnp.where(low, turned, spectra)
    for o in range(2):

        def mix(i, totals):
            x1, x2 = w1[i, o * 32 : (o + 1) * 32, :], w2[i, o * 32 : (o + 1) * 32, :]
            return tuple(
                total
                + x1 * s_rows[0, pl.ds(z * 16 + i, 1), :]
                + x2 * s_rows[1, pl.ds(z * 16 + i, 1), :]
                for z, total in enumerate(totals)
            )

        totals = lax.fori_loop(0, 16, mix, (jnp.zeros((32, 128), F32),) * 4, unroll=4)
        for z, total in enumerate(totals):
            for k in range(2):
                mixpart[o * 2 + k, z * 16 : (z + 1) * 16, :] = total[k * 16 : (k + 1) * 16].astype(BF16)
    for r in (OWN, FAR):
        for to_n, device in along_z(r):
            pltpu.make_async_remote_copy(
                mixpart.at[to_n], mix_in.at[at_z], mix_send.at[r], mix_recv.at[r],
                device_id=device, device_id_type=MESH,
            ).start()
    mix_in[at_z] = mixpart[n]

    wait_blocks(cots_in, 4, cots_recv.at[FAR])
    wait_blocks(cots_in, 3, cots_recv.at[OWN])
    low = low_lanes((64, 128))
    for o in range(4):
        both = cots_in[o].astype(F32) + cots_in[4 + o].astype(F32)
        rounded = (both * 8.0).astype(BF16)
        d = rounded.astype(F32)
        turned = halves_swapped(d)
        d1[:, o * 16 : (o + 1) * 16, :] = d.reshape(4, 16, 128)
        d2[:, o * 16 : (o + 1) * 16, :] = jnp.where(low, turned, -turned).reshape(4, 16, 128)

    def gradient(i, _):
        x1, x2 = w1[i], w2[i]
        for z in range(4):
            terms = (x1 * d1[z] + x2 * d2[z]).reshape(8, 8, 128)
            sg[pl.ds(pl.multiple_of((z * 16 + i) * 8, 8), 8), :] = jnp.sum(terms, axis=0)
        return 0

    lax.fori_loop(0, 16, gradient, 0, unroll=4)
    sums = sg[pl.ds(0, 64, stride=8), :]
    for k in range(1, 8):
        sums += sg[pl.ds(k, 64, stride=8), :]
    modes[COT, half] = (sums * 0.125).astype(BF16)
    cot_back = pltpu.make_async_remote_copy(
        modes.at[COT, half], modes.at[COT, half], mx_send, mx_recv, device_id=partner, device_id_type=MESH
    )
    cot_back.start()

    def rows_of_y(a, r):
        m = modes[a, modes_of[r]]
        zero = jnp.zeros_like(m)
        wide = jnp.concatenate(
            [jnp.concatenate([m, zero], axis=1), jnp.concatenate([zero, m], axis=1)], axis=0
        )
        rows = lax.dot_general(fy[...], wide, (((1,), (1,)), ((), ())), preferred_element_type=F32)
        send2[a, modes_of[r]] = rows.astype(BF16).reshape(GROUP, 16, 128)
        all_to_all(a, r, send2, recv2, s2_send, s2_recv)

    def mixed_rows(r):
        wait_blocks(mix_in, 4 if r == FAR else 3, mix_recv.at[r])
        first = modes_of[r] * 4
        total = mix_in[first].astype(F32)
        for k in range(1, 4):
            total += mix_in[first + k].astype(F32)
        modes[FIELD, modes_of[r]] = total.astype(BF16)
        rows_of_y(FIELD, r)

    rows_of_y(COT, OWN)

    mixed_rows(OWN)
    cot_back.wait_recv()
    rows_of_y(COT, FAR)
    mixed_rows(FAR)

    def weight_gradient(i, _):
        for o in range(2):
            total = jnp.zeros((32, 128), F32)
            for z in range(4):
                row = pl.ds(z * 16 + i, 1)
                outs = slice(o * 32, (o + 1) * 32)
                total += a1[row, :] * d1[z, outs, :] + a2[row, :] * d2[z, outs, :]
            wg[pl.ds(pl.multiple_of(i * 64 + o * 32, 32), 32), :] = total
        return 0

    lax.fori_loop(0, 16, weight_gradient, 0, unroll=2)

    for a, out in ((COT, grad_out), (FIELD, back_out)):
        blocks = t32.reshape(GROUP, 2, 16, 128)
        for r in range(2):
            wait_blocks(recv2.at[a, 0], GROUP - 1, s2_recv.at[a, r])
        for h in range(2):
            blocks[:, h] = recv2[a, h].astype(F32)

        def turn_back(y8, _):
            block = t32[pl.ds(y8, 128, stride=8), :].T
            for y2 in range(2):
                for z in range(4):
                    at = (y2 * 4 + z) * 16
                    xm[a, pl.ds(z * 16 + y2 * 8 + y8, 16, stride=64), :] = block[at : at + 16]
            return 0

        lax.fori_loop(0, 8, turn_back, 0, unroll=True)
        out[...] = xm[a].astype(BF16)

    for a in range(2):
        for r in range(2):
            wait_blocks(send1.at[a, 0], GROUP - 1, s1_send.at[a, r])
            wait_blocks(send2.at[a, 0], GROUP - 1, s2_send.at[a, r])
    field_part.wait_send()
    cot_back.wait_send()
    for r, count in ((FAR, 4), (OWN, 3)):
        wait_blocks(cots_in, count, cots_send.at[r])
        wait_blocks(mix_in, count, mix_send.at[r])


def exchange(cot, field, weight, fx, fy):
    hbm = pl.BlockSpec(memory_space=pltpu.HBM)
    vmem = pl.BlockSpec(memory_space=pltpu.VMEM)
    dma = pltpu.SemaphoreType.DMA
    return pl.pallas_call(
        exchange_kernel,
        out_shape=(
            pltpu.VMEM((ROWS, 128), BF16),
            pltpu.VMEM((ROWS, 128), BF16),
            pltpu.VMEM((ROWS, 128), F32),
        ),
        in_specs=[hbm] * 5,
        out_specs=(vmem,) * 3,
        scratch_shapes=[
            pltpu.VMEM((2, ROWS, X), BF16),
            pltpu.VMEM((X, 128), BF16),
            pltpu.VMEM((GROUP * 16, 256), BF16),
            pltpu.VMEM((16, 64, 128), BF16),
            pltpu.VMEM((16, 64, 128), F32),
            pltpu.VMEM((16, 64, 128), F32),
            pltpu.VMEM((2, ROWS, 128), F32),
            pltpu.VMEM((ROWS, 128), F32),
            pltpu.VMEM((2, 2, GROUP, 16, 128), BF16),
            pltpu.VMEM((2, 2, GROUP, 16, 128), BF16),
            pltpu.VMEM((2, 2, 64, 128), BF16),
            pltpu.VMEM((64, 128), F32),
            pltpu.VMEM((64, 128), BF16),
            pltpu.VMEM((2, 64, 128), F32),
            pltpu.VMEM((64, 128), F32),
            pltpu.VMEM((64, 128), F32),
            pltpu.VMEM((4, 64, 128), BF16),
            pltpu.VMEM((8, 64, 128), BF16),
            pltpu.VMEM((8, 64, 128), BF16),
            pltpu.VMEM((4, 64, 128), F32),
            pltpu.VMEM((4, 64, 128), F32),
            pltpu.VMEM((512, 128), F32),
            pltpu.VMEM((2, 2, 64, 128), BF16),
            pltpu.VMEM((2, 2, GROUP, 16, 128), BF16),
            pltpu.VMEM((2, 2, GROUP, 16, 128), BF16),
            dma((11,)),
            dma((2, 2)),
            dma((2, 2)),
            dma,
            dma,
            dma((2,)),
            dma((2,)),
            dma((2,)),
            dma((2,)),
            dma,
            dma,
            dma((2, 2)),
            dma((2, 2)),
        ],
        compiler_params=pltpu.CompilerParams(
            collective_id=0, has_side_effects=True, vmem_limit_bytes=44 << 20
        ),
    )(*(pltpu.with_memory_space_constraint(a, pltpu.HBM) for a in (cot, field, weight, fx, fy)))


def rows_kernel(grad, back, wg, ix, fgrad, wg_out, out, buf, sem):
    chunk = ROWS // 4
    copies = [pltpu.make_async_copy(wg, wg_out, sem.at[8])]
    copies[0].start()
    for a, (src, dst) in enumerate(((grad, fgrad), (back, out))):
        for c in range(4):
            rows = pl.ds(c * chunk, chunk)
            buf[a, rows, :] = jnp.dot(
                src[rows, :], ix[...], preferred_element_type=F32
            ).astype(BF16)
            copy = pltpu.make_async_copy(buf.at[a, rows], dst.at[rows], sem.at[a * 4 + c])
            copy.start()
            copies.append(copy)
    for copy in copies:
        copy.wait()


def rows_back(grad, back, wg, ix):
    hbm = pl.BlockSpec(memory_space=pltpu.HBM)
    vmem = pl.BlockSpec(memory_space=pltpu.VMEM)
    rows = jax.ShapeDtypeStruct((ROWS, X), BF16)
    return pl.pallas_call(
        rows_kernel,
        out_shape=(rows, jax.ShapeDtypeStruct((ROWS, 128), F32), rows),
        in_specs=[vmem] * 4,
        out_specs=(hbm,) * 3,
        scratch_shapes=[
            pltpu.VMEM((2, ROWS, X), BF16),
            pltpu.SemaphoreType.DMA((9,)),
        ],
        compiler_params=pltpu.CompilerParams(vmem_limit_bytes=44 << 20),
    )(grad, back, wg, ix)


def solution(mesh):
    forward_x, inverse_x, forward_y = tables()

    def body(field, spectral_weight, cotangent):
        shape = field.shape
        grad, back, weight_grad = exchange(
            cotangent.reshape(ROWS, X),
            field.reshape(ROWS, X),
            spectral_weight.reshape(16, 64, 128),
            jnp.asarray(forward_x),
            jnp.asarray(forward_y),
        )
        field_grad, weight_grad, output = rows_back(
            grad, back, weight_grad, jnp.asarray(inverse_x)
        )
        return (
            output.reshape(shape),
            weight_grad.reshape(16, 64, 1, 128),
            field_grad.reshape(shape),
        )

    spec = P("narrow", None, "wide", None)
    return jax.shard_map(
        body, mesh=mesh, in_specs=(spec,) * 3, out_specs=(spec,) * 3, check_vma=False
    )
```

```python
import math

import jax
import jax.numpy as jnp
import ml_dtypes
import numpy as np
from jax import lax
from jax.experimental import pallas as pl
from jax.experimental.pallas import tpu as pltpu
from jax.sharding import PartitionSpec as P

X = 1024
Y = 1024
MX = 64
MY = 64
GROUP = 32
ROWS = 1024
MESH = pl.DeviceIdType.MESH
F32 = jnp.float32
BF16 = jnp.bfloat16


def mode_of(group, half):
    return (group // 2) * 4 + half * 2 + group % 2


def tables():
    step = np.float32(2.0 * math.pi / X)
    group = np.arange(GROUP)
    k = np.stack([mode_of(group, h) for h in range(2)], axis=1)
    ax = ((np.arange(X)[:, None, None] * k[None]) % X).astype(np.float32) * step
    fx = np.stack([np.cos(ax), -np.sin(ax)], axis=-1).reshape(X, 2 * MX)
    forward_x = (fx / np.float32(32)).astype(ml_dtypes.bfloat16)
    inverse_x = np.ascontiguousarray((fx / np.float32(4)).astype(ml_dtypes.bfloat16).T)
    m = np.arange(MY)
    q = np.where(m < MY // 2, m, m - MY + Y)
    ay = ((np.arange(Y)[:, None] * q[None]) % Y).astype(np.float32) * step
    cos, sin = np.cos(ay), np.sin(ay)
    fy = np.stack([np.concatenate([cos, -sin], 1), np.concatenate([sin, cos], 1)], 0)
    fy = (fy / np.float32(32)).astype(ml_dtypes.bfloat16)
    halves = []
    for h in range(2):
        y = 16 * mode_of(group, h)[:, None] + np.arange(16)[None]
        part = fy[:, y, :].reshape(2, GROUP, 2, 8, 2 * MY)
        halves.append(part.transpose(1, 0, 3, 2, 4).reshape(GROUP * 16, 4 * MY))
    return forward_x, inverse_x, np.stack(halves)


def halves_swapped(a):
    return pltpu.roll(a, MY, a.ndim - 1)


def low_lanes(shape):
    return lax.broadcasted_iota(jnp.int32, shape, len(shape) - 1) < MY


def far_first():
    offsets = [(dy, dx, dc) for dy in range(4) for dx in range(4) for dc in range(2)]
    return sorted(offsets[1:], key=lambda o: -(min(o[0], 4 - o[0]) + min(o[1], 4 - o[1])))


COT, FIELD = 0, 1


def rows_from_blocks(blocks, t32, xm):
    parts = t32.reshape(GROUP, 2, 16, 128)
    for h in range(2):
        parts[:, h] = blocks[h].astype(F32)

    def turn_back(y8, _):
        block = t32[pl.ds(y8, 128, stride=8), :].T
        for y2 in range(2):
            for z in range(4):
                at = (y2 * 4 + z) * 16
                xm[pl.ds(z * 16 + y2 * 8 + y8, 16, stride=64), :] = block[at : at + 16]
        return 0

    lax.fori_loop(0, 8, turn_back, 0, unroll=True)


FAR, OWN = 0, 1


def exchange_kernel(
    cot, field, weight, fx_hbm, fy_hbm,
    grad_out, back_out, wg,
    rows_in, fx, fy, wt, w1, w2, xm, t32, send1, recv1, part, part_own, part_in, s_rows,
    a1, a2, mixpart, mix_in, cots_in, d1, d2, sg, modes, send2, recv2,
    in_sem, s1_send, s1_recv, px_send, px_recv, mix_send, mix_recv, cots_send, cots_recv,
    mx_send, mx_recv, s2_send, s2_recv,
):
    w = lax.axis_index("wide")
    n = lax.axis_index("narrow")
    at_y, at_x, half, core = lax.div(w, 16), lax.rem(lax.div(w, 4), 4), lax.rem(lax.div(w, 2), 2), lax.rem(w, 2)
    g = lax.div(w, 4) * 2 + core
    at_z = half * 4 + n
    partner = {"wide": w + 2 - 4 * half, "narrow": n}

    def member(offset):
        dy, dx, dc = offset
        chip = lax.rem(at_y + dy, 4) * 4 + lax.rem(at_x + dx, 4)
        to_core = lax.rem(core + dc, 2)
        return chip * 2 + to_core, {"wide": chip * 4 + half * 2 + to_core, "narrow": n}

    modes_of = (1 - half, half)

    def along_z(r):
        wide = w + 2 * (modes_of[r] - half)
        for i in (0, 1, 3, 2) if r == FAR else (2, 1, 3):
            to_n = lax.rem(n + i, 4)
            yield to_n, {"wide": wide, "narrow": to_n}

    barrier = pltpu.get_barrier_semaphore()
    for offset in far_first():
        pl.semaphore_signal(barrier, 1, device_id=member(offset)[1], device_id_type=MESH)
    for r in (FAR, OWN):
        for _, device in along_z(r):
            pl.semaphore_signal(barrier, 1, device_id=device, device_id_type=MESH)

    chunk = ROWS // 4
    copies = []
    copies.append(pltpu.make_async_copy(fx_hbm, fx, in_sem.at[8]))
    for a, src in enumerate((cot, field)):
        for c in range(4):
            rows = pl.ds(c * chunk, chunk)
            copies.append(
                pltpu.make_async_copy(src.at[rows], rows_in.at[a, rows], in_sem.at[a * 4 + c])
            )
    fy_copy = pltpu.make_async_copy(fy_hbm.at[half], fy, in_sem.at[9])
    wt_copy = pltpu.make_async_copy(weight, wt, in_sem.at[10])
    for copy in copies:
        copy.start()
    fy_copy.start()
    wt_copy.start()

    copies[0].wait()

    def all_to_all(a, r, sent, received, send_sem, recv_sem):
        src, dst = sent.at[a, modes_of[r]], received.at[a, modes_of[r]]
        for offset in far_first():
            other, device = member(offset)
            pltpu.make_async_remote_copy(
                src.at[other], dst.at[g], send_sem.at[a, r], recv_sem.at[a, r],
                device_id=device, device_id_type=MESH,
            ).start()
        dst[g] = src[g]

    def wait_blocks(ref, count, sem):
        block = ref.at[pl.ds(0, count)]
        pltpu.make_async_copy(block, block, sem).wait()

    def x_transform(a):
        for c in range(4):
            copies[1 + a * 4 + c].wait()
            rows = pl.ds(c * chunk, chunk)
            xm[a, rows, :] = jnp.dot(rows_in[a, rows, :], fx[...], preferred_element_type=F32)

    def blocks_for_modes(a):
        def turn(y8, _):
            pieces = [
                xm[a, pl.ds(z * 16 + y2 * 8 + y8, 16, stride=64), :]
                for y2 in range(2)
                for z in range(4)
            ]
            t32[pl.ds(y8, 128, stride=8), :] = jnp.concatenate(pieces, axis=0).T
            return 0

        lax.fori_loop(0, 8, turn, 0, unroll=True)
        blocks = t32[...].astype(BF16).reshape(GROUP, 2, 16, 128)
        for h in range(2):
            send1[a, h] = blocks[:, h]

    x_transform(COT)
    blocks_for_modes(COT)
    x_transform(FIELD)
    pl.semaphore_wait(barrier, GROUP - 1 + 7)
    all_to_all(COT, FAR, send1, recv1, s1_send, s1_recv)
    blocks_for_modes(FIELD)
    all_to_all(FIELD, FAR, send1, recv1, s1_send, s1_recv)
    all_to_all(COT, OWN, send1, recv1, s1_send, s1_recv)
    all_to_all(FIELD, OWN, send1, recv1, s1_send, s1_recv)

    wt_copy.wait()

    def spread(i, _):
        both = wt[i].astype(F32)
        turned = halves_swapped(both)
        low = low_lanes(both.shape)
        w1[i] = jnp.where(low, both, turned)
        w2[i] = jnp.where(low, turned, both)
        return 0

    lax.fori_loop(0, 16, spread, 0, unroll=2)
    fy_copy.wait()

    def sums_over_y(a, r):
        wait_blocks(recv1.at[a, 0], GROUP - 1, s1_recv.at[a, r])
        block = recv1[a, modes_of[r]].reshape(GROUP * 16, 128)
        both = lax.dot_general(
            block, fy[...], (((0,), (0,)), ((), ())), preferred_element_type=F32
        )
        return both[:64, :128] + both[64:, 128:]

    def cots_along_z(r):
        part[COT, r] = sums_over_y(COT, r).astype(BF16)
        for _, device in along_z(r):
            pltpu.make_async_remote_copy(
                part.at[COT, r], cots_in.at[at_z], cots_send.at[r], cots_recv.at[r],
                device_id=device, device_id_type=MESH,
            ).start()

    cots_along_z(FAR)

    part[FIELD, FAR] = sums_over_y(FIELD, FAR).astype(BF16)
    field_part = pltpu.make_async_remote_copy(
        part.at[FIELD, FAR], part_in, px_send, px_recv, device_id=partner, device_id_type=MESH
    )
    field_part.start()

    cots_along_z(OWN)
    cots_in[at_z] = part[COT, OWN]
    part_own[...] = sums_over_y(FIELD, OWN)

    field_part.wait_recv()
    low = low_lanes((64, 128))
    spectra = (part_own[...] + part_in[...].astype(F32)).astype(BF16).astype(F32)
    turned = halves_swapped(spectra)
    s_rows[0] = spectra
    s_rows[1] = jnp.where(low, -turned, turned)
    a1[...] = jnp.where(low, spectra, turned)
    a2[...] = jnp.where(low, turned, spectra)
    for o in range(2):

        def mix(i, totals):
            x1, x2 = w1[i, o * 32 : (o + 1) * 32, :], w2[i, o * 32 : (o + 1) * 32, :]
            return tuple(
                total
                + x1 * s_rows[0, pl.ds(z * 16 + i, 1), :]
                + x2 * s_rows[1, pl.ds(z * 16 + i, 1), :]
                for z, total in enumerate(totals)
            )

        totals = lax.fori_loop(0, 16, mix, (jnp.zeros((32, 128), F32),) * 4, unroll=4)
        for z, total in enumerate(totals):
            for k in range(2):
                mixpart[o * 2 + k, z * 16 : (z + 1) * 16, :] = total[k * 16 : (k + 1) * 16].astype(BF16)
    for r in (OWN, FAR):
        for to_n, device in along_z(r):
            pltpu.make_async_remote_copy(
                mixpart.at[to_n], mix_in.at[at_z], mix_send.at[r], mix_recv.at[r],
                device_id=device, device_id_type=MESH,
            ).start()
    mix_in[at_z] = mixpart[n]

    wait_blocks(cots_in, 4, cots_recv.at[FAR])
    wait_blocks(cots_in, 3, cots_recv.at[OWN])
    low = low_lanes((64, 128))
    for o in range(4):
        both = cots_in[o].astype(F32) + cots_in[4 + o].astype(F32)
        rounded = (both * 8.0).astype(BF16)
        d = rounded.astype(F32)
        turned = halves_swapped(d)
        d1[:, o * 16 : (o + 1) * 16, :] = d.reshape(4, 16, 128)
        d2[:, o * 16 : (o + 1) * 16, :] = jnp.where(low, turned, -turned).reshape(4, 16, 128)

    def gradient(i, _):
        x1, x2 = w1[i], w2[i]
        for z in range(4):
            terms = (x1 * d1[z] + x2 * d2[z]).reshape(8, 8, 128)
            sg[pl.ds(pl.multiple_of((z * 16 + i) * 8, 8), 8), :] = jnp.sum(terms, axis=0)
        return 0

    lax.fori_loop(0, 16, gradient, 0, unroll=4)
    sums = sg[pl.ds(0, 64, stride=8), :]
    for k in range(1, 8):
        sums += sg[pl.ds(k, 64, stride=8), :]
    modes[COT, half] = (sums * 0.125).astype(BF16)
    cot_back = pltpu.make_async_remote_copy(
        modes.at[COT, half], modes.at[COT, half], mx_send, mx_recv, device_id=partner, device_id_type=MESH
    )
    cot_back.start()

    def rows_of_y(a, r):
        m = modes[a, modes_of[r]]
        zero = jnp.zeros_like(m)
        wide = jnp.concatenate(
            [jnp.concatenate([m, zero], axis=1), jnp.concatenate([zero, m], axis=1)], axis=0
        )
        rows = lax.dot_general(fy[...], wide, (((1,), (1,)), ((), ())), preferred_element_type=F32)
        send2[a, modes_of[r]] = rows.astype(BF16).reshape(GROUP, 16, 128)
        all_to_all(a, r, send2, recv2, s2_send, s2_recv)

    def mixed_rows(r):
        wait_blocks(mix_in, 4 if r == FAR else 3, mix_recv.at[r])
        first = modes_of[r] * 4
        total = mix_in[first].astype(F32)
        for k in range(1, 4):
            total += mix_in[first + k].astype(F32)
        modes[FIELD, modes_of[r]] = total.astype(BF16)
        rows_of_y(FIELD, r)

    rows_of_y(COT, OWN)

    mixed_rows(OWN)
    cot_back.wait_recv()
    rows_of_y(COT, FAR)
    mixed_rows(FAR)

    def weight_gradient(i, _):
        for o in range(2):
            total = jnp.zeros((32, 128), F32)
            for z in range(4):
                row = pl.ds(z * 16 + i, 1)
                outs = slice(o * 32, (o + 1) * 32)
                total += a1[row, :] * d1[z, outs, :] + a2[row, :] * d2[z, outs, :]
            wg[pl.ds(pl.multiple_of(i * 64 + o * 32, 32), 32), :] = total
        return 0

    lax.fori_loop(0, 16, weight_gradient, 0, unroll=2)

    for r in range(2):
        wait_blocks(recv2.at[COT, 0], GROUP - 1, s2_recv.at[COT, r])
    rows_from_blocks(recv2.at[COT], t32, xm.at[COT])
    grad_out[...] = xm[COT].astype(BF16)
    for r in range(2):
        wait_blocks(recv2.at[FIELD, 0], GROUP - 1, s2_recv.at[FIELD, r])
    back_out[...] = recv2[FIELD]

    for a in range(2):
        for r in range(2):
            wait_blocks(send1.at[a, 0], GROUP - 1, s1_send.at[a, r])
            wait_blocks(send2.at[a, 0], GROUP - 1, s2_send.at[a, r])
    field_part.wait_send()
    cot_back.wait_send()
    for r, count in ((FAR, 4), (OWN, 3)):
        wait_blocks(cots_in, count, cots_send.at[r])
        wait_blocks(mix_in, count, mix_send.at[r])


def exchange(cot, field, weight, fx, fy):
    hbm = pl.BlockSpec(memory_space=pltpu.HBM)
    vmem = pl.BlockSpec(memory_space=pltpu.VMEM)
    dma = pltpu.SemaphoreType.DMA
    return pl.pallas_call(
        exchange_kernel,
        out_shape=(
            pltpu.VMEM((ROWS, 128), BF16),
            pltpu.VMEM((2, GROUP, 16, 128), BF16),
            pltpu.VMEM((ROWS, 128), F32),
        ),
        in_specs=[hbm] * 5,
        out_specs=(vmem,) * 3,
        scratch_shapes=[
            pltpu.VMEM((2, ROWS, X), BF16),
            pltpu.VMEM((X, 128), BF16),
            pltpu.VMEM((GROUP * 16, 256), BF16),
            pltpu.VMEM((16, 64, 128), BF16),
            pltpu.VMEM((16, 64, 128), F32),
            pltpu.VMEM((16, 64, 128), F32),
            pltpu.VMEM((2, ROWS, 128), F32),
            pltpu.VMEM((ROWS, 128), F32),
            pltpu.VMEM((2, 2, GROUP, 16, 128), BF16),
            pltpu.VMEM((2, 2, GROUP, 16, 128), BF16),
            pltpu.VMEM((2, 2, 64, 128), BF16),
            pltpu.VMEM((64, 128), F32),
            pltpu.VMEM((64, 128), BF16),
            pltpu.VMEM((2, 64, 128), F32),
            pltpu.VMEM((64, 128), F32),
            pltpu.VMEM((64, 128), F32),
            pltpu.VMEM((4, 64, 128), BF16),
            pltpu.VMEM((8, 64, 128), BF16),
            pltpu.VMEM((8, 64, 128), BF16),
            pltpu.VMEM((4, 64, 128), F32),
            pltpu.VMEM((4, 64, 128), F32),
            pltpu.VMEM((512, 128), F32),
            pltpu.VMEM((2, 2, 64, 128), BF16),
            pltpu.VMEM((2, 2, GROUP, 16, 128), BF16),
            pltpu.VMEM((2, 2, GROUP, 16, 128), BF16),
            dma((11,)),
            dma((2, 2)),
            dma((2, 2)),
            dma,
            dma,
            dma((2,)),
            dma((2,)),
            dma((2,)),
            dma((2,)),
            dma,
            dma,
            dma((2, 2)),
            dma((2, 2)),
        ],
        compiler_params=pltpu.CompilerParams(
            collective_id=0, has_side_effects=True, vmem_limit_bytes=44 << 20
        ),
    )(*(pltpu.with_memory_space_constraint(a, pltpu.HBM) for a in (cot, field, weight, fx, fy)))


def rows_kernel(grad, back, wg, ix, fgrad, wg_out, out, buf, t32, xm, sem):
    chunk = ROWS // 4
    copies = [pltpu.make_async_copy(wg, wg_out, sem.at[8])]
    copies[0].start()
    for a, (src, dst) in enumerate(((grad, fgrad), (xm, out))):
        if a == FIELD:
            rows_from_blocks(back, t32, xm)
        for c in range(4):
            rows = pl.ds(c * chunk, chunk)
            buf[a, rows, :] = jnp.dot(
                src[rows, :].astype(BF16), ix[...], preferred_element_type=F32
            ).astype(BF16)
            copy = pltpu.make_async_copy(buf.at[a, rows], dst.at[rows], sem.at[a * 4 + c])
            copy.start()
            copies.append(copy)
    for copy in copies:
        copy.wait()


def rows_back(grad, back, wg, ix):
    hbm = pl.BlockSpec(memory_space=pltpu.HBM)
    vmem = pl.BlockSpec(memory_space=pltpu.VMEM)
    rows = jax.ShapeDtypeStruct((ROWS, X), BF16)
    return pl.pallas_call(
        rows_kernel,
        out_shape=(rows, jax.ShapeDtypeStruct((ROWS, 128), F32), rows),
        in_specs=[vmem] * 4,
        out_specs=(hbm,) * 3,
        scratch_shapes=[
            pltpu.VMEM((2, ROWS, X), BF16),
            pltpu.VMEM((ROWS, 128), F32),
            pltpu.VMEM((ROWS, 128), F32),
            pltpu.SemaphoreType.DMA((9,)),
        ],
        compiler_params=pltpu.CompilerParams(vmem_limit_bytes=44 << 20),
    )(grad, back, wg, ix)


def solution(mesh):
    forward_x, inverse_x, forward_y = tables()

    def body(field, spectral_weight, cotangent):
        shape = field.shape
        grad, back, weight_grad = exchange(
            cotangent.reshape(ROWS, X),
            field.reshape(ROWS, X),
            spectral_weight.reshape(16, 64, 128),
            jnp.asarray(forward_x),
            jnp.asarray(forward_y),
        )
        field_grad, weight_grad, output = rows_back(
            grad, back, weight_grad, jnp.asarray(inverse_x)
        )
        return (
            output.reshape(shape),
            weight_grad.reshape(16, 64, 1, 128),
            field_grad.reshape(shape),
        )

    spec = P("narrow", None, "wide", None)
    return jax.shard_map(
        body, mesh=mesh, in_specs=(spec,) * 3, out_specs=(spec,) * 3, check_vma=False
    )
```

```python
import math

import jax
import jax.numpy as jnp
import ml_dtypes
import numpy as np
from jax import lax
from jax.experimental import pallas as pl
from jax.experimental.pallas import tpu as pltpu
from jax.sharding import PartitionSpec as P

X = 1024
Y = 1024
MX = 64
MY = 64
GROUP = 32
ROWS = 1024
MESH = pl.DeviceIdType.MESH
F32 = jnp.float32
BF16 = jnp.bfloat16


def mode_of(group, half):
    return (group // 2) * 4 + half * 2 + group % 2


def tables():
    step = np.float32(2.0 * math.pi / X)
    group = np.arange(GROUP)
    k = np.stack([mode_of(group, h) for h in range(2)], axis=1)
    ax = ((np.arange(X)[:, None, None] * k[None]) % X).astype(np.float32) * step
    fx = np.stack([np.cos(ax), -np.sin(ax)], axis=-1).reshape(X, 2 * MX)
    forward_x = (fx / np.float32(32)).astype(ml_dtypes.bfloat16)
    inverse_x = np.ascontiguousarray((fx / np.float32(4)).astype(ml_dtypes.bfloat16).T)
    m = np.arange(MY)
    q = np.where(m < MY // 2, m, m - MY + Y)
    ay = ((np.arange(Y)[:, None] * q[None]) % Y).astype(np.float32) * step
    cos, sin = np.cos(ay), np.sin(ay)
    fy = np.stack([np.concatenate([cos, -sin], 1), np.concatenate([sin, cos], 1)], 0)
    fy = (fy / np.float32(32)).astype(ml_dtypes.bfloat16)
    halves = []
    for h in range(2):
        y = 16 * mode_of(group, h)[:, None] + np.arange(16)[None]
        part = fy[:, y, :].reshape(2, GROUP, 2, 8, 2 * MY)
        halves.append(part.transpose(1, 0, 3, 2, 4).reshape(GROUP * 16, 4 * MY))
    return forward_x, inverse_x, np.stack(halves)


def halves_swapped(a):
    return pltpu.roll(a, MY, a.ndim - 1)


def low_lanes(shape):
    return lax.broadcasted_iota(jnp.int32, shape, len(shape) - 1) < MY


def far_first():
    offsets = [(dy, dx, dc) for dy in range(4) for dx in range(4) for dc in range(2)]
    return sorted(offsets[1:], key=lambda o: -(min(o[0], 4 - o[0]) + min(o[1], 4 - o[1])))


COT, FIELD = 0, 1


def rows_from_blocks(blocks, t32, xm):
    parts = t32.reshape(GROUP, 2, 16, 128)
    for h in range(2):
        parts[:, h] = blocks[h].astype(F32)

    def turn_back(y8, _):
        block = t32[pl.ds(y8, 128, stride=8), :].T
        for y2 in range(2):
            for z in range(4):
                at = (y2 * 4 + z) * 16
                xm[pl.ds(z * 16 + y2 * 8 + y8, 16, stride=64), :] = block[at : at + 16]
        return 0

    lax.fori_loop(0, 8, turn_back, 0, unroll=True)


FAR, OWN = 0, 1


def exchange_kernel(
    cot, field, weight, fx_hbm, fy_hbm,
    grad_out, back_out, wg,
    rows_in, fx, fy, wt, w1, w2, xm, t32, send1, recv1, part, part_own, part_in, s_rows,
    a1, a2, mixpart, mix_in, cots_in, d1, d2, sg, modes, send2, recv2,
    in_sem, s1_send, s1_recv, px_send, px_recv, mix_send, mix_recv, cots_send, cots_recv,
    mx_send, mx_recv, s2_send, s2_recv,
):
    w = lax.axis_index("wide")
    n = lax.axis_index("narrow")
    at_y, at_x, half, core = lax.div(w, 16), lax.rem(lax.div(w, 4), 4), lax.rem(lax.div(w, 2), 2), lax.rem(w, 2)
    g = lax.div(w, 4) * 2 + core
    at_z = half * 4 + n
    partner = {"wide": w + 2 - 4 * half, "narrow": n}

    def member(offset):
        dy, dx, dc = offset
        chip = lax.rem(at_y + dy, 4) * 4 + lax.rem(at_x + dx, 4)
        to_core = lax.rem(core + dc, 2)
        return chip * 2 + to_core, {"wide": chip * 4 + half * 2 + to_core, "narrow": n}

    modes_of = (1 - half, half)

    def along_z(r):
        wide = w + 2 * (modes_of[r] - half)
        for i in (0, 1, 3, 2) if r == FAR else (2, 1, 3):
            to_n = lax.rem(n + i, 4)
            yield to_n, {"wide": wide, "narrow": to_n}

    barrier = pltpu.get_barrier_semaphore()
    for offset in far_first():
        pl.semaphore_signal(barrier, 1, device_id=member(offset)[1], device_id_type=MESH)
    for r in (FAR, OWN):
        for _, device in along_z(r):
            pl.semaphore_signal(barrier, 1, device_id=device, device_id_type=MESH)

    chunk = ROWS // 4
    copies = []
    copies.append(pltpu.make_async_copy(fx_hbm, fx, in_sem.at[8]))
    for a, src in enumerate((cot, field)):
        for c in range(4):
            rows = pl.ds(c * chunk, chunk)
            copies.append(
                pltpu.make_async_copy(src.at[rows], rows_in.at[a, rows], in_sem.at[a * 4 + c])
            )
    fy_copy = pltpu.make_async_copy(fy_hbm.at[half], fy, in_sem.at[9])
    wt_copy = pltpu.make_async_copy(weight, wt, in_sem.at[10])
    for copy in copies:
        copy.start()
    fy_copy.start()
    wt_copy.start()

    copies[0].wait()

    def all_to_all(a, r, sent, received, send_sem, recv_sem):
        src, dst = sent.at[a, modes_of[r]], received.at[a, modes_of[r]]
        for offset in far_first():
            other, device = member(offset)
            pltpu.make_async_remote_copy(
                src.at[other], dst.at[g], send_sem.at[a, r], recv_sem.at[a, r],
                device_id=device, device_id_type=MESH,
            ).start()
        dst[g] = src[g]

    def wait_blocks(ref, count, sem):
        block = ref.at[pl.ds(0, count)]
        pltpu.make_async_copy(block, block, sem).wait()

    def x_transform(a):
        for c in range(4):
            copies[1 + a * 4 + c].wait()
            rows = pl.ds(c * chunk, chunk)
            xm[a, rows, :] = jnp.dot(rows_in[a, rows, :], fx[...], preferred_element_type=F32)

    def blocks_for_modes(a):
        def turn(y8, _):
            pieces = [
                xm[a, pl.ds(z * 16 + y2 * 8 + y8, 16, stride=64), :]
                for y2 in range(2)
                for z in range(4)
            ]
            t32[pl.ds(y8, 128, stride=8), :] = jnp.concatenate(pieces, axis=0).T
            return 0

        lax.fori_loop(0, 8, turn, 0, unroll=True)
        blocks = t32[...].astype(BF16).reshape(GROUP, 2, 16, 128)
        for h in range(2):
            send1[a, h] = blocks[:, h]

    x_transform(COT)
    blocks_for_modes(COT)
    x_transform(FIELD)
    pl.semaphore_wait(barrier, GROUP - 1 + 7)
    all_to_all(COT, FAR, send1, recv1, s1_send, s1_recv)
    blocks_for_modes(FIELD)
    all_to_all(FIELD, FAR, send1, recv1, s1_send, s1_recv)
    all_to_all(COT, OWN, send1, recv1, s1_send, s1_recv)
    all_to_all(FIELD, OWN, send1, recv1, s1_send, s1_recv)

    wt_copy.wait()

    def spread(i, _):
        both = wt[i].astype(F32)
        turned = halves_swapped(both)
        low = low_lanes(both.shape)
        w1[i] = jnp.where(low, both, turned)
        w2[i] = jnp.where(low, turned, both)
        return 0

    lax.fori_loop(0, 16, spread, 0, unroll=2)
    fy_copy.wait()

    def sums_over_y(a, r):
        wait_blocks(recv1.at[a, 0], GROUP - 1, s1_recv.at[a, r])
        block = recv1[a, modes_of[r]].reshape(GROUP * 16, 128)
        both = lax.dot_general(
            block, fy[...], (((0,), (0,)), ((), ())), preferred_element_type=F32
        )
        return both[:64, :128] + both[64:, 128:]

    def cots_along_z(r):
        part[COT, r] = sums_over_y(COT, r).astype(BF16)
        for _, device in along_z(r):
            pltpu.make_async_remote_copy(
                part.at[COT, r], cots_in.at[at_z], cots_send.at[r], cots_recv.at[r],
                device_id=device, device_id_type=MESH,
            ).start()

    cots_along_z(FAR)

    part[FIELD, FAR] = sums_over_y(FIELD, FAR).astype(BF16)
    field_part = pltpu.make_async_remote_copy(
        part.at[FIELD, FAR], part_in, px_send, px_recv, device_id=partner, device_id_type=MESH
    )
    field_part.start()

    cots_along_z(OWN)
    cots_in[at_z] = part[COT, OWN]
    part_own[...] = sums_over_y(FIELD, OWN)

    field_part.wait_recv()
    low = low_lanes((64, 128))
    spectra = (part_own[...] + part_in[...].astype(F32)).astype(BF16).astype(F32)
    turned = halves_swapped(spectra)
    s_rows[0] = spectra
    s_rows[1] = jnp.where(low, -turned, turned)
    a1[...] = jnp.where(low, spectra, turned)
    a2[...] = jnp.where(low, turned, spectra)
    for o in range(2):

        def mix(i, totals):
            x1, x2 = w1[i, o * 32 : (o + 1) * 32, :], w2[i, o * 32 : (o + 1) * 32, :]
            return tuple(
                total
                + x1 * s_rows[0, pl.ds(z * 16 + i, 1), :]
                + x2 * s_rows[1, pl.ds(z * 16 + i, 1), :]
                for z, total in enumerate(totals)
            )

        totals = lax.fori_loop(0, 16, mix, (jnp.zeros((32, 128), F32),) * 4, unroll=4)
        for z, total in enumerate(totals):
            for k in range(2):
                mixpart[o * 2 + k, z * 16 : (z + 1) * 16, :] = total[k * 16 : (k + 1) * 16].astype(BF16)
    for r in (OWN, FAR):
        for to_n, device in along_z(r):
            pltpu.make_async_remote_copy(
                mixpart.at[to_n], mix_in.at[at_z], mix_send.at[r], mix_recv.at[r],
                device_id=device, device_id_type=MESH,
            ).start()
    mix_in[at_z] = mixpart[n]

    wait_blocks(cots_in, 4, cots_recv.at[FAR])
    wait_blocks(cots_in, 3, cots_recv.at[OWN])
    low = low_lanes((64, 128))
    for o in range(4):
        both = cots_in[o].astype(F32) + cots_in[4 + o].astype(F32)
        rounded = (both * 8.0).astype(BF16)
        d = rounded.astype(F32)
        turned = halves_swapped(d)
        d1[:, o * 16 : (o + 1) * 16, :] = d.reshape(4, 16, 128)
        d2[:, o * 16 : (o + 1) * 16, :] = jnp.where(low, turned, -turned).reshape(4, 16, 128)

    def gradient(i, _):
        x1, x2 = w1[i], w2[i]
        for z in range(4):
            terms = (x1 * d1[z] + x2 * d2[z]).reshape(8, 8, 128)
            sg[pl.ds(pl.multiple_of((z * 16 + i) * 8, 8), 8), :] = jnp.sum(terms, axis=0)
        return 0

    lax.fori_loop(0, 16, gradient, 0, unroll=4)
    sums = sg[pl.ds(0, 64, stride=8), :]
    for k in range(1, 8):
        sums += sg[pl.ds(k, 64, stride=8), :]
    modes[COT, half] = (sums * 0.125).astype(BF16)
    cot_back = pltpu.make_async_remote_copy(
        modes.at[COT, half], modes.at[COT, half], mx_send, mx_recv, device_id=partner, device_id_type=MESH
    )
    cot_back.start()

    def rows_of_y(a, r):
        m = modes[a, modes_of[r]]
        zero = jnp.zeros_like(m)
        wide = jnp.concatenate(
            [jnp.concatenate([m, zero], axis=1), jnp.concatenate([zero, m], axis=1)], axis=0
        )
        rows = lax.dot_general(fy[...], wide, (((1,), (1,)), ((), ())), preferred_element_type=F32)
        send2[a, modes_of[r]] = rows.astype(BF16).reshape(GROUP, 16, 128)
        all_to_all(a, r, send2, recv2, s2_send, s2_recv)

    def mixed_rows(r):
        wait_blocks(mix_in, 4 if r == FAR else 3, mix_recv.at[r])
        first = modes_of[r] * 4
        total = mix_in[first].astype(F32)
        for k in range(1, 4):
            total += mix_in[first + k].astype(F32)
        modes[FIELD, modes_of[r]] = total.astype(BF16)
        rows_of_y(FIELD, r)

    rows_of_y(COT, OWN)

    mixed_rows(OWN)
    cot_back.wait_recv()
    rows_of_y(COT, FAR)
    mixed_rows(FAR)

    def weight_gradient(i, _):
        for o in range(2):
            total = jnp.zeros((32, 128), F32)
            for z in range(4):
                row = pl.ds(z * 16 + i, 1)
                outs = slice(o * 32, (o + 1) * 32)
                total += a1[row, :] * d1[z, outs, :] + a2[row, :] * d2[z, outs, :]
            wg[pl.ds(pl.multiple_of(i * 64 + o * 32, 32), 32), :] = total
        return 0

    lax.fori_loop(0, 16, weight_gradient, 0, unroll=2)

    for r in range(2):
        wait_blocks(recv2.at[COT, 0], GROUP - 1, s2_recv.at[COT, r])
    rows_from_blocks(recv2.at[COT], t32, xm.at[COT])
    grad_out[...] = xm[COT].astype(BF16)
    for r in range(2):
        wait_blocks(recv2.at[FIELD, 0], GROUP - 1, s2_recv.at[FIELD, r])
    back_out[...] = recv2[FIELD]

    for a in range(2):
        for r in range(2):
            wait_blocks(send1.at[a, 0], GROUP - 1, s1_send.at[a, r])
            wait_blocks(send2.at[a, 0], GROUP - 1, s2_send.at[a, r])
    field_part.wait_send()
    cot_back.wait_send()
    for r, count in ((FAR, 4), (OWN, 3)):
        wait_blocks(cots_in, count, cots_send.at[r])
        wait_blocks(mix_in, count, mix_send.at[r])


def exchange(cot, field, weight, fx, fy):
    hbm = pl.BlockSpec(memory_space=pltpu.HBM)
    vmem = pl.BlockSpec(memory_space=pltpu.VMEM)
    dma = pltpu.SemaphoreType.DMA
    return pl.pallas_call(
        exchange_kernel,
        out_shape=(
            pltpu.VMEM((ROWS, 128), BF16),
            pltpu.VMEM((2, GROUP, 16, 128), BF16),
            pltpu.VMEM((ROWS, 128), F32),
        ),
        in_specs=[hbm] * 5,
        out_specs=(vmem,) * 3,
        scratch_shapes=[
            pltpu.VMEM((2, ROWS, X), BF16),
            pltpu.VMEM((X, 128), BF16),
            pltpu.VMEM((GROUP * 16, 256), BF16),
            pltpu.VMEM((16, 64, 128), BF16),
            pltpu.VMEM((16, 64, 128), F32),
            pltpu.VMEM((16, 64, 128), F32),
            pltpu.VMEM((2, ROWS, 128), F32),
            pltpu.VMEM((ROWS, 128), F32),
            pltpu.VMEM((2, 2, GROUP, 16, 128), BF16),
            pltpu.VMEM((2, 2, GROUP, 16, 128), BF16),
            pltpu.VMEM((2, 2, 64, 128), BF16),
            pltpu.VMEM((64, 128), F32),
            pltpu.VMEM((64, 128), BF16),
            pltpu.VMEM((2, 64, 128), F32),
            pltpu.VMEM((64, 128), F32),
            pltpu.VMEM((64, 128), F32),
            pltpu.VMEM((4, 64, 128), BF16),
            pltpu.VMEM((8, 64, 128), BF16),
            pltpu.VMEM((8, 64, 128), BF16),
            pltpu.VMEM((4, 64, 128), F32),
            pltpu.VMEM((4, 64, 128), F32),
            pltpu.VMEM((512, 128), F32),
            pltpu.VMEM((2, 2, 64, 128), BF16),
            pltpu.VMEM((2, 2, GROUP, 16, 128), BF16),
            pltpu.VMEM((2, 2, GROUP, 16, 128), BF16),
            dma((11,)),
            dma((2, 2)),
            dma((2, 2)),
            dma,
            dma,
            dma((2,)),
            dma((2,)),
            dma((2,)),
            dma((2,)),
            dma,
            dma,
            dma((2, 2)),
            dma((2, 2)),
        ],
        compiler_params=pltpu.CompilerParams(
            collective_id=0, has_side_effects=True, vmem_limit_bytes=44 << 20
        ),
    )(*(pltpu.with_memory_space_constraint(a, pltpu.HBM) for a in (cot, field, weight, fx, fy)))


def rows_kernel(grad, back, wg, ix, fgrad, wg_out, out, buf, t32, xm, sem):
    chunk = ROWS // 8
    copies = [pltpu.make_async_copy(wg, wg_out, sem.at[16])]
    copies[0].start()
    for a, (src, dst) in enumerate(((grad, fgrad), (xm, out))):
        if a == FIELD:
            rows_from_blocks(back, t32, xm)
        for c in range(8):
            rows = pl.ds(c * chunk, chunk)
            buf[a, rows, :] = jnp.dot(
                src[rows, :].astype(BF16), ix[...], preferred_element_type=F32
            ).astype(BF16)
            copy = pltpu.make_async_copy(buf.at[a, rows], dst.at[rows], sem.at[a * 8 + c])
            copy.start()
            copies.append(copy)
    for copy in copies:
        copy.wait()


def rows_back(grad, back, wg, ix):
    hbm = pl.BlockSpec(memory_space=pltpu.HBM)
    vmem = pl.BlockSpec(memory_space=pltpu.VMEM)
    rows = jax.ShapeDtypeStruct((ROWS, X), BF16)
    return pl.pallas_call(
        rows_kernel,
        out_shape=(rows, jax.ShapeDtypeStruct((ROWS, 128), F32), rows),
        in_specs=[vmem] * 4,
        out_specs=(hbm,) * 3,
        scratch_shapes=[
            pltpu.VMEM((2, ROWS, X), BF16),
            pltpu.VMEM((ROWS, 128), F32),
            pltpu.VMEM((ROWS, 128), F32),
            pltpu.SemaphoreType.DMA((17,)),
        ],
        compiler_params=pltpu.CompilerParams(vmem_limit_bytes=44 << 20),
    )(grad, back, wg, ix)


def solution(mesh):
    forward_x, inverse_x, forward_y = tables()

    def body(field, spectral_weight, cotangent):
        shape = field.shape
        grad, back, weight_grad = exchange(
            cotangent.reshape(ROWS, X),
            field.reshape(ROWS, X),
            spectral_weight.reshape(16, 64, 128),
            jnp.asarray(forward_x),
            jnp.asarray(forward_y),
        )
        field_grad, weight_grad, output = rows_back(
            grad, back, weight_grad, jnp.asarray(inverse_x)
        )
        return (
            output.reshape(shape),
            weight_grad.reshape(16, 64, 1, 128),
            field_grad.reshape(shape),
        )

    spec = P("narrow", None, "wide", None)
    return jax.shard_map(
        body, mesh=mesh, in_specs=(spec,) * 3, out_specs=(spec,) * 3, check_vma=False
    )
```
